128 devices in a mesh: dom: 32 (over y, x, core), rep: 4 (over z).
Axes of the slice: x: 4, y: 4, z: 4, core: 2. Of those that a mesh axis runs over, the one named last changes fastest.
Arguments:
- node_feat: bfloat16 [4, 8192, 512], P('rep', 'dom'), may hold values from -6 to 6
- edge_feat: bfloat16 [4, 65536, 512], P('rep', 'dom'), may hold values from -6 to 6
- node_cot: bfloat16 [4, 8192, 512], P('rep', 'dom'), may hold values from -6 to 6
- edge_cot: bfloat16 [4, 65536, 512], P('rep', 'dom'), may hold values from -6 to 6
- edge_in_w: bfloat16 [1536, 512], replicated, may hold values from -0.15625 to 0.15625
- edge_bias: float32 [512], replicated, may hold values from -3 to 3
- edge_out_w: bfloat16 [512, 512], replicated, may hold values from -0.25 to 0.25
- edge_gain: float32 [512], replicated, may hold values from 0.25 to 1.75
- node_in_w: bfloat16 [1024, 512], replicated, may hold values from -0.1875 to 0.1875
- node_bias: float32 [512], replicated, may hold values from -3 to 3
- node_out_w: bfloat16 [512, 512], replicated, may hold values from -0.25 to 0.25
- node_gain: float32 [512], replicated, may hold values from 0.25 to 1.75
- senders: int32 [65536], P('dom'), may hold values from 0 to 1279, as said below
- receivers: int32 [65536], P('dom'), may hold values from 0 to 255
- send_rows: int32 [1024, 32], P('dom'), may hold values from 0 to 255
- live_edges: int32 [32], P('dom'), may hold values from 1 to 2048, 40960 in all
Outputs:
- grad_nodes: bfloat16 [4, 8192, 512], P('rep', 'dom')
- grad_edges: bfloat16 [4, 65536, 512], P('rep', 'dom')
- grad_matrices: float32 [3584, 512], P('dom')
- grad_vectors: float32 [4, 512], replicated
The draws below stay inside these ranges and needn't reach their ends.
Inputs may be any that keep to these rules, and one draw needn't show every extreme that they name: `senders`: rows below 256 are local nodes; row 256 + q * 32 + j is slot j of the list that region q sends to this region. `receivers`: A local node of the edge's own region. `send_rows`: row q * 32 + p lists local nodes of region q that region p receives; nodes may repeat. `live_edges`: some region uses all its slots; the used slots come first.
All inputs are finite; a program needn't handle non-finite values. No bound on the sum of `live_edges` on one device may be relied on, other than what follows from the above.
Results may differ from the reference program's by a relative error of at most 0.014.
Values may be sent and summed in bfloat16 or wider, within the bound.
No kernel may reach another device: no remote copies, remote signals or barrier semaphores. Data moves between devices by JAX's collectives and lax.ppermute only.
A program may use at most 192 MiB of HBM per device.

```python
import math
import jax
import jax.numpy as jnp
import numpy as np
from jax import lax

D = 512
EDGE_DEV = 2048
NODE_DEV = 256
CAP = 32
HALO = 1280
NODES = 8192
EDGES = 65536
SAMPLES = 4
N_DOM = 32


def draw_senders(key, part):
    key = jax.random.fold_in(key, 7)
    keys = jax.random.split(key, 5)
    slot_index = jnp.arange(EDGES, dtype=jnp.int32)
    region = slot_index // EDGE_DEV
    offset = slot_index - region * EDGE_DEV
    kind_pick = jax.random.randint(keys[0], (EDGES,), 0, 20)
    local_row = jax.random.randint(keys[1], (EDGES,), 0, NODE_DEV)
    steps_table = jnp.array([1, -1, 2, -2, 4, -4], dtype=jnp.int32)
    near_pick = jax.random.randint(keys[2], (EDGES,), 0, 6)
    near_region = jnp.mod(region + steps_table[near_pick], N_DOM)
    far_region = jax.random.randint(keys[3], (EDGES,), 0, N_DOM)
    column = jax.random.randint(keys[4], (EDGES,), 0, CAP)
    source = jnp.where(kind_pick < 19, near_region, far_region)
    remote_row = NODE_DEV + source * CAP + column
    rows = jnp.where(kind_pick < 15, local_row, remote_row)
    rows = jnp.where(offset == 0, 0, rows)
    rows = jnp.where(offset == 1, HALO - 1, rows)
    return rows.astype(jnp.int32)


def place_ends(values, key, smallest, top_value):
    place = [jax.random.randint(jax.random.fold_in(key, axis), (), 0, length) for axis, length in enumerate(values.shape)]
    longest = values.shape.index(max(values.shape))
    neighbour = place[:longest] + [(place[longest] + 1) % values.shape[longest]] + place[longest + 1:]
    return values.at[tuple(place)].set(smallest).at[tuple(neighbour)].set(top_value)


def shard_levels(own_key, shape, cuts, least, top_value):
    factor_of = 1.0
    for axis_at, parts in cuts:
        draws = jax.random.uniform(jax.random.fold_in(jax.random.fold_in(own_key, 6), axis_at), (parts,), jnp.float32, least / len(cuts), top_value / len(cuts))
        factor_of = factor_of * jnp.repeat(jnp.exp(draws), shape[axis_at] // parts).reshape((-1,) + (1,) * (len(shape) - 1 - axis_at))
    return factor_of


def length_profile(number_of, total, most, skew):
    loads = [(1 << 20) // math.isqrt(rank ** skew) + 1 for rank in range(2, number_of + 1)]
    spare, holding = total - most - (number_of - 1), [1] * (number_of - 1)
    while spare > 0:
        free = [i for i in range(number_of - 1) if holding[i] < most]
        whole, budget = sum([loads[i] for i in free]), spare
        for i in free:
            more = min(most - holding[i], max(1, budget * loads[i] // whole), spare)
            holding[i] = holding[i] + more
            spare = spare - more
    return np.array([most] + holding)


def ragged_sizes(key, number_of, total, most, lean):
    if number_of == 2:
        one = jax.random.randint(key, (), max(1, total - most), min(most, total - 1) + 1)
        return jnp.stack([one, total - one])
    tallies = jnp.asarray(length_profile(number_of, total, most, lean), jnp.int32)
    couples = (number_of - 1) // 2
    giver, sink = tallies[1:1 + 2 * couples:2], tallies[2:2 + 2 * couples:2]
    room = jnp.minimum(giver - 1, most - sink)
    shifted = jax.random.randint(jax.random.fold_in(key, 1), (couples,), 0, 1 << 20) % (room + 1)
    tallies = tallies.at[1:1 + 2 * couples:2].set(giver - shifted).at[2:2 + 2 * couples:2].set(sink + shifted)
    return tallies[jax.random.permutation(jax.random.fold_in(key, 2), number_of)]


def bell_draw(rng, extent, deviation, limit, pieces=(), held_as=jnp.bfloat16):
    entries = deviation * jax.random.normal(rng, extent, jnp.float32)
    if pieces:
        entries = entries * shard_levels(rng, extent, pieces, -0.22, 0.18)
    return jnp.clip(entries, -limit, limit).astype(held_as)


def setup_inputs(seed: int = 0) -> dict:
    streams_of = jax.random.split(jax.random.key(seed), 17)
    return {
        "node_feat": bell_draw(streams_of[0], (SAMPLES, NODES, D), 1.0, 6.0, ((0, 4), (1, 32))),
        "edge_feat": bell_draw(streams_of[1], (SAMPLES, EDGES, D), 1.0, 6.0, ((0, 4), (1, 32))),
        "node_cot": bell_draw(streams_of[2], (SAMPLES, NODES, D), 1.0, 6.0, ((0, 4), (1, 32))),
        "edge_cot": bell_draw(streams_of[3], (SAMPLES, EDGES, D), 1.0, 6.0, ((0, 4), (1, 32))),
        "edge_in_w": bell_draw(streams_of[4], (3 * D, D), (3 * D) ** -0.5, 0.15625),
        "edge_bias": bell_draw(streams_of[5], (D,), 0.5, 3.0, (), jnp.float32),
        "edge_out_w": bell_draw(streams_of[6], (D, D), D ** -0.5, 0.25),
        "edge_gain": jnp.clip(1.0 + 0.15 * jax.random.normal(streams_of[7], (D,), jnp.float32), 0.25, 1.75),
        "node_in_w": bell_draw(streams_of[8], (2 * D, D), (2 * D) ** -0.5, 0.1875),
        "node_bias": bell_draw(streams_of[9], (D,), 0.5, 3.0, (), jnp.float32),
        "node_out_w": bell_draw(streams_of[10], (D, D), D ** -0.5, 0.25),
        "node_gain": jnp.clip(1.0 + 0.15 * jax.random.normal(streams_of[11], (D,), jnp.float32), 0.25, 1.75),
        "senders": draw_senders(jax.random.fold_in(streams_of[16], 71), 0),
        "receivers": place_ends(jax.random.randint(streams_of[13], (EDGES,), 0, NODE_DEV), jax.random.fold_in(streams_of[13], 1), 0, NODE_DEV - 1).astype(jnp.int32),
        "send_rows": place_ends(jax.random.randint(streams_of[14], (N_DOM * N_DOM, CAP), 0, NODE_DEV), jax.random.fold_in(streams_of[14], 1), 0, NODE_DEV - 1).astype(jnp.int32),
        "live_edges": ragged_sizes(streams_of[15], N_DOM, N_DOM * EDGE_DEV * 5 // 8, EDGE_DEV, 2).astype(jnp.int32),
    }


epsilon = 1e-05

def silu_slope(value):
    sig = jax.nn.sigmoid(value)
    return sig * (1.0 + value * (1.0 - sig))

def norm_forward(value):
    center = value - lax.optimization_barrier(jnp.mean(value, axis=-1, keepdims=True))
    recip = lax.rsqrt(lax.optimization_barrier(jnp.mean(center * center, axis=-1, keepdims=True)) + epsilon)
    return (center * recip, recip)

def norm_backward(upper, normed, recip):
    return recip * (upper - lax.optimization_barrier(jnp.mean(upper, axis=-1, keepdims=True)) - normed * lax.optimization_barrier(jnp.mean(upper * normed, axis=-1, keepdims=True)))

def reference(node_feat, edge_feat, node_cot, edge_cot, edge_in_w, edge_bias, edge_out_w, edge_gain, node_in_w, node_bias, node_out_w, node_gain, senders, receivers, send_rows, live_edges):
    width = node_feat.shape[2]
    total_nodes = node_feat.shape[1]
    slot_index = jnp.arange(EDGES, dtype=jnp.int32)
    region = slot_index // EDGE_DEV
    offset = slot_index - region * EDGE_DEV
    halo_pos = jnp.clip(senders - NODE_DEV, 0, N_DOM * CAP - 1).astype(jnp.int32)
    source = halo_pos // CAP
    column = halo_pos - source * CAP
    listed = send_rows[source * N_DOM + region, column]
    global_snd = jnp.where(senders < NODE_DEV, region * NODE_DEV + senders, source * NODE_DEV + listed).astype(jnp.int32)
    global_rcv = (region * NODE_DEV + receivers).astype(jnp.int32)
    live_mask = (offset < live_edges[region]).astype(jnp.float32)[:, None]

    def one_sample(operands):
        nodes, edges, node_grad_in, edge_grad_in = operands
        inputs = jnp.concatenate([edges, nodes[global_snd], nodes[global_rcv]], axis=1)
        hidden = jnp.dot(inputs, edge_in_w, preferred_element_type=jnp.float32) + edge_bias
        act = jax.nn.silu(hidden).astype(jnp.bfloat16)
        pre = jnp.dot(act, edge_out_w, preferred_element_type=jnp.float32)
        normed, recip = norm_forward(pre)
        message = (live_mask * normed * edge_gain).astype(jnp.bfloat16)
        agg = jax.ops.segment_sum(message.astype(jnp.float32), global_rcv, total_nodes).astype(jnp.bfloat16)
        node_in = jnp.concatenate([nodes, agg], axis=1)
        node_hidden = jnp.dot(node_in, node_in_w, preferred_element_type=jnp.float32) + node_bias
        node_act = jax.nn.silu(node_hidden).astype(jnp.bfloat16)
        node_pre = jnp.dot(node_act, node_out_w, preferred_element_type=jnp.float32)
        node_normed, node_recip = norm_forward(node_pre)
        upstream = node_grad_in.astype(jnp.float32)
        node_pre_grad = norm_backward(upstream * node_gain, node_normed, node_recip).astype(jnp.bfloat16)
        node_hidden_grad = (jnp.dot(node_pre_grad, node_out_w.T, preferred_element_type=jnp.float32) * silu_slope(node_hidden)).astype(jnp.bfloat16)
        node_in_grad = jnp.dot(node_hidden_grad, node_in_w.T, preferred_element_type=jnp.float32)
        agg_grad = node_in_grad[:, width:]
        message_grad = live_mask * (edge_grad_in.astype(jnp.float32) + agg_grad[global_rcv])
        pre_grad = norm_backward(message_grad * edge_gain, normed, recip).astype(jnp.bfloat16)
        hidden_grad = (jnp.dot(pre_grad, edge_out_w.T, preferred_element_type=jnp.float32) * silu_slope(hidden)).astype(jnp.bfloat16)
        inputs_grad = jnp.dot(hidden_grad, edge_in_w.T, preferred_element_type=jnp.float32)
        grad_edges = (edge_grad_in.astype(jnp.float32) + inputs_grad[:, :width]).astype(jnp.bfloat16)
        grad_nodes = upstream + node_in_grad[:, :width]
        grad_nodes = grad_nodes + jax.ops.segment_sum(inputs_grad[:, width:2 * width], global_snd, total_nodes)
        grad_nodes = grad_nodes + jax.ops.segment_sum(inputs_grad[:, 2 * width:], global_rcv, total_nodes)
        matrices = jnp.concatenate([jnp.dot(inputs.T, hidden_grad, preferred_element_type=jnp.float32), jnp.dot(act.T, pre_grad, preferred_element_type=jnp.float32), jnp.dot(node_in.T, node_hidden_grad, preferred_element_type=jnp.float32), jnp.dot(node_act.T, node_pre_grad, preferred_element_type=jnp.float32)], axis=0)
        vectors = jnp.stack([lax.optimization_barrier(jnp.sum(hidden_grad.astype(jnp.float32), axis=0)), lax.optimization_barrier(jnp.sum(message_grad * normed, axis=0)), lax.optimization_barrier(jnp.sum(node_hidden_grad.astype(jnp.float32), axis=0)), lax.optimization_barrier(jnp.sum(upstream * node_normed, axis=0))])
        return (grad_nodes.astype(jnp.bfloat16), grad_edges, matrices, vectors)
    grad_nodes, grad_edges, matrices, vectors = lax.map(one_sample, (node_feat, edge_feat, node_cot, edge_cot))
    return (grad_nodes, grad_edges, lax.optimization_barrier(jnp.sum(matrices, axis=0)), lax.optimization_barrier(jnp.sum(vectors, axis=0)))
```

```python
import functools

import jax
import jax.numpy as jnp
from jax import lax
from jax.experimental import pallas as pl
from jax.experimental.pallas import tpu as pltpu
from jax.sharding import PartitionSpec as P

epsilon = 1e-05
f32 = jnp.float32
bf16 = jnp.bfloat16
NT = (((1,), (1,)), ((), ()))
TN = (((0,), (0,)), ((), ()))
VMEM_LIMIT = 58 * 1024 * 1024


def mm(a, b):
    return jnp.dot(a, b, preferred_element_type=f32)


def mm_nt(a, b):
    return lax.dot_general(a, b, NT, preferred_element_type=f32)


def mm_tn(a, b):
    return lax.dot_general(a, b, TN, preferred_element_type=f32)


def params():
    return pltpu.CompilerParams(vmem_limit_bytes=VMEM_LIMIT)


def one_hot_t(row, first, count):
    ids = lax.broadcasted_iota(jnp.int32, (count, row.shape[1]), 0) + first
    return jnp.where(ids == row, 1.0, 0.0).astype(bf16)


def columns(row):
    k = row.shape[1]
    parts = [
        jnp.transpose(jnp.broadcast_to(row[:, i : i + 128], (128, 128))) for i in range(0, k, 128)
    ]
    return jnp.concatenate(parts, axis=0)


def one_hot(column, first, count):
    lane = lax.broadcasted_iota(jnp.int32, column.shape, 1)
    parts = [
        jnp.where(column == lane + (first + i), 1.0, 0.0).astype(bf16)
        for i in range(0, count, 128)
    ]
    return jnp.concatenate(parts, axis=1)


def sigmoid(value):
    return 0.5 * jnp.tanh(0.5 * value) + 0.5


def normalise(value):
    center = value - jnp.mean(value, axis=-1, keepdims=True)
    recip = lax.rsqrt(jnp.mean(center * center, axis=-1, keepdims=True) + epsilon)
    return center * recip, recip


def norm_backward(upper, normed, recip):
    return recip * (
        upper
        - jnp.mean(upper, axis=-1, keepdims=True)
        - normed * jnp.mean(upper * normed, axis=-1, keepdims=True)
    )


def send_kernel(rows_ref, nodes_ref, out_ref):
    n = nodes_ref.shape[0]
    out_ref[...] = mm_tn(one_hot_t(rows_ref[...], 0, n), nodes_ref[...]).astype(bf16)


def edge_forward_step(
    c,
    chunk,
    edges_ref,
    nodes_ref,
    arrived_ref,
    ein_ref,
    ebias_ref,
    eout_ref,
    egain_ref,
    snd_ref,
    rcv_ref,
    table_scr,
    act_scr,
    slope_scr,
    normed_scr,
    recip_scr,
    agg_scr,
):
    n, width = nodes_ref.shape
    remote = arrived_ref.shape[0]

    @pl.when(c == 0)
    def _():
        w_s = ein_ref[width : 2 * width, :]
        table_scr[:n, :] = mm(nodes_ref[...], w_s).astype(bf16)
        table_scr[n : n + remote, :] = mm(arrived_ref[...], w_s).astype(bf16)
        table_scr[n + remote :, :] = mm(nodes_ref[...], ein_ref[2 * width :, :]).astype(bf16)
        agg_scr[...] = jnp.zeros_like(agg_scr)

    here = pl.ds(pl.multiple_of(c * chunk, chunk), chunk)
    snd = snd_ref[pl.ds(c, 1), :]
    rcv = rcv_ref[pl.ds(c, 1), :]
    picks = jnp.concatenate(
        [
            one_hot(columns(snd), 0, n + remote),
            one_hot(columns(jnp.bitwise_and(rcv, 0xFFFF)), 0, n),
        ],
        axis=1,
    )
    hidden = mm(edges_ref[...], ein_ref[:width, :]) + mm(picks, table_scr[...]) + ebias_ref[...]
    s = sigmoid(hidden)
    act = (hidden * s).astype(bf16)
    act_scr[here, :] = act
    slope_scr[here, :] = (s * (1.0 + hidden * (1.0 - s))).astype(slope_scr.dtype)
    normed, recip = normalise(mm(act, eout_ref[...]))
    normed_scr[here, :] = normed.astype(normed_scr.dtype)
    recip_scr[here, :] = recip
    message = (normed * egain_ref[...]).astype(bf16)
    agg_scr[...] += mm(one_hot_t(rcv, 0, n), message)


def main_kernel(
    chunk,
    snd_ref,
    rcv_ref,
    edges_ref,
    cot_ref,
    nodes_ref,
    ncot_ref,
    arrived_ref,
    ein_ref,
    ebias_ref,
    eout_ref,
    egain_ref,
    nin_ref,
    nbias_ref,
    nout_ref,
    ngain_ref,
    grad_ref,
    sent_ref,
    base_ref,
    mats_ref,
    vecs_ref,
    table_scr,
    act_scr,
    slope_scr,
    normed_scr,
    recip_scr,
    agg_scr,
    agg_grad_scr,
    x_scr,
    hg_scr,
    pg_scr,
    ns_scr,
):
    step = pl.program_id(0)
    n, width = nodes_ref.shape
    remote = arrived_ref.shape[0]
    n_chunks = snd_ref.shape[0]
    nsteps = 2 * n_chunks

    @pl.when(step < n_chunks)
    def _():
        edge_forward_step(
            step,
            chunk,
            edges_ref,
            nodes_ref,
            arrived_ref,
            ein_ref,
            ebias_ref,
            eout_ref,
            egain_ref,
            snd_ref,
            rcv_ref,
            table_scr,
            act_scr,
            slope_scr,
            normed_scr,
            recip_scr,
            agg_scr,
        )
        here = pl.ds(pl.multiple_of(step * chunk, chunk), chunk)
        x_scr[here, :] = edges_ref[...]

    @pl.when(step == n_chunks - 1)
    def _():
        nodes = nodes_ref[...]
        agg = agg_scr[...].astype(bf16)
        hidden = mm(nodes, nin_ref[:width, :]) + mm(agg, nin_ref[width:, :]) + nbias_ref[...]
        s = sigmoid(hidden)
        act = (hidden * s).astype(bf16)
        normed, recip = normalise(mm(act, nout_ref[...]))
        upstream = ncot_ref[...].astype(f32)
        pre_grad = norm_backward(upstream * ngain_ref[...], normed, recip).astype(bf16)
        hidden_grad = (
            mm_nt(pre_grad, nout_ref[...]) * (s * (1.0 + hidden * (1.0 - s)))
        ).astype(bf16)
        agg_grad_scr[...] = mm_nt(hidden_grad, nin_ref[width:, :]).astype(bf16)
        base_ref[...] = upstream + mm_nt(hidden_grad, nin_ref[:width, :])
        mats_ref[4 * width : 5 * width, :] = mm_tn(nodes, hidden_grad).astype(bf16)
        mats_ref[5 * width : 6 * width, :] = mm_tn(agg, hidden_grad).astype(bf16)
        mats_ref[6 * width :, :] = mm_tn(act, pre_grad).astype(bf16)
        vecs_ref[...] = jnp.zeros_like(vecs_ref)
        vecs_ref[2:3, :] = jnp.sum(hidden_grad.astype(f32), axis=0, keepdims=True)
        vecs_ref[3:4, :] = jnp.sum(upstream * normed, axis=0, keepdims=True)

    @pl.when(step >= n_chunks)
    def _():
        c = step - n_chunks
        here = pl.ds(pl.multiple_of(c * chunk, chunk), chunk)
        rcv = columns(rcv_ref[pl.ds(c, 1), :])
        cot = cot_ref[...].astype(f32)
        gathered = mm(one_hot(rcv, 0, n), agg_grad_scr[...])
        live = rcv[:, :1] < 0x10000
        message_grad = jnp.where(live, cot + gathered, 0.0)
        normed = normed_scr[here, :].astype(f32)
        vecs_ref[1:2, :] += jnp.sum(message_grad * normed, axis=0, keepdims=True)
        pre_grad = norm_backward(message_grad * egain_ref[...], normed, recip_scr[here, :]).astype(
            bf16
        )
        pg_scr[here, :] = pre_grad
        hidden_grad = (
            mm_nt(pre_grad, eout_ref[...]) * slope_scr[here, :].astype(f32)
        ).astype(bf16)
        hg_scr[here, :] = hidden_grad
        vecs_ref[0:1, :] += jnp.sum(hidden_grad.astype(f32), axis=0, keepdims=True)
        grad_ref[...] = (cot + mm_nt(hidden_grad, ein_ref[:width, :])).astype(bf16)

    @pl.when(step == nsteps - 1)
    def _():
        mats_ref[3 * width : 4 * width, :] = mm_tn(act_scr[...], pg_scr[...]).astype(bf16)
        mats_ref[:width, :] = mm_tn(x_scr[...], hg_scr[...]).astype(bf16)
        w_s = ein_ref[width : 2 * width, :]
        w_r = ein_ref[2 * width :, :]
        snd = jnp.concatenate([snd_ref[c : c + 1, :] for c in range(n_chunks)], axis=1)
        rcv = jnp.concatenate([rcv_ref[c : c + 1, :] for c in range(n_chunks)], axis=1)
        local = mm(one_hot_t(snd, 0, n), hg_scr[...]).astype(bf16)
        ns_scr[:n, :] = local
        received = mm(one_hot_t(rcv, 0, n), hg_scr[...]).astype(bf16)
        tile = 256 if remote % 256 == 0 else remote

        @pl.loop(0, remote // tile)
        def _(i):
            at = pl.multiple_of(i * tile, tile)
            part = mm(one_hot_t(snd, n + at, tile), hg_scr[...]).astype(bf16)
            sent_ref[pl.ds(at, tile), :] = part

        base_ref[...] += mm_nt(local, w_s) + mm_nt(received, w_r)
        mats_ref[width : 2 * width, :] = (
            mm_tn(nodes_ref[...], local) + mm_tn(arrived_ref[...], sent_ref[...])
        ).astype(bf16)
        mats_ref[2 * width : 3 * width, :] = mm_tn(nodes_ref[...], received).astype(bf16)


def finish_kernel(rows_ref, returned_ref, ein_ref, base_ref, out_ref):
    n, width = base_ref.shape
    own = mm(one_hot_t(rows_ref[...], 0, n), returned_ref[...]).astype(bf16)
    out_ref[...] = (base_ref[...] + mm_nt(own, ein_ref[width : 2 * width, :])).astype(bf16)


def sum_kernel(parts_ref, out_ref):
    out_ref[...] = jnp.sum(parts_ref[...].astype(f32), axis=0)


def cost(flops, moved):
    return pl.CostEstimate(flops=flops, bytes_accessed=moved, transcendentals=0)


def shards(
    node_feat,
    edge_feat,
    node_cot,
    edge_cot,
    edge_in_w,
    edge_bias,
    edge_out_w,
    edge_gain,
    node_in_w,
    node_bias,
    node_out_w,
    node_gain,
    senders,
    receivers,
    send_rows,
    live_edges,
):
    nodes = node_feat[0]
    edges = edge_feat[0]
    n, width = nodes.shape
    count = edges.shape[0]
    regions, cap = send_rows.shape
    remote = regions * cap
    chunk = min(512, count)
    n_chunks = count // chunk
    listed = send_rows.reshape(1, remote)

    outgoing = pl.pallas_call(
        send_kernel,
        out_shape=jax.ShapeDtypeStruct((remote, width), bf16),
        compiler_params=params(),
    )(listed, nodes)
    arrived = lax.all_to_all(
        outgoing.reshape(regions, cap, width), "dom", split_axis=0, concat_axis=0, tiled=True
    ).reshape(remote, width)

    live = jnp.arange(count, dtype=jnp.int32) < live_edges[0]
    rcv = jnp.where(live, receivers, receivers + 0x10000).reshape(n_chunks, chunk)
    snd = senders.reshape(n_chunks, chunk)

    def whole(shape):
        return pl.BlockSpec(shape, lambda i: (0,) * len(shape))

    def fwd(i):
        return (jnp.minimum(i, n_chunks - 1), 0)

    def bwd(i):
        return (jnp.maximum(i - n_chunks, 0), 0)

    rows = edge_in_w.shape[0] + edge_out_w.shape[0] + node_in_w.shape[0] + node_out_w.shape[0]
    grad_edges, sent, base, mats, vecs = pl.pallas_call(
        functools.partial(main_kernel, chunk),
        grid=(2 * n_chunks,),
        in_specs=[
            whole((n_chunks, chunk)),
            whole((n_chunks, chunk)),
            pl.BlockSpec((chunk, width), fwd),
            pl.BlockSpec((chunk, width), bwd),
            whole((n, width)),
            whole((n, width)),
            whole((remote, width)),
            whole(edge_in_w.shape),
            whole((1, width)),
            whole(edge_out_w.shape),
            whole((1, width)),
            whole(node_in_w.shape),
            whole((1, width)),
            whole(node_out_w.shape),
            whole((1, width)),
        ],
        out_specs=[
            pl.BlockSpec((chunk, width), bwd),
            whole((remote, width)),
            whole((n, width)),
            whole((rows, width)),
            whole((8, width)),
        ],
        out_shape=[
            jax.ShapeDtypeStruct((count, width), bf16),
            jax.ShapeDtypeStruct((remote, width), bf16),
            jax.ShapeDtypeStruct((n, width), f32),
            jax.ShapeDtypeStruct((rows, width), bf16),
            jax.ShapeDtypeStruct((8, width), f32),
        ],
        scratch_shapes=[
            pltpu.VMEM((2 * n + remote, width), bf16),
            pltpu.VMEM((count, width), bf16),
            pltpu.VMEM((count, width), f32),
            pltpu.VMEM((count, width), f32),
            pltpu.VMEM((count, 1), f32),
            pltpu.VMEM((n, width), f32),
            pltpu.VMEM((n, width), bf16),
            pltpu.VMEM((count, width), bf16),
            pltpu.VMEM((count, width), bf16),
            pltpu.VMEM((count, width), bf16),
            pltpu.VMEM((n, width), bf16),
        ],
        compiler_params=params(),
        cost_estimate=cost(16_000_000_000, 16_000_000),
    )(
        snd,
        rcv,
        edges,
        edge_cot[0],
        nodes,
        node_cot[0],
        arrived,
        edge_in_w,
        edge_bias.reshape(1, width),
        edge_out_w,
        edge_gain.reshape(1, width),
        node_in_w,
        node_bias.reshape(1, width),
        node_out_w,
        node_gain.reshape(1, width),
    )

    share = rows // regions
    parts = lax.all_to_all(
        mats.reshape(regions, share, width), "dom", split_axis=0, concat_axis=0, tiled=True
    )
    returned = lax.all_to_all(
        sent.reshape(regions, cap, width), "dom", split_axis=0, concat_axis=0, tiled=True
    ).reshape(remote, width)
    vector_total = lax.psum(vecs[:4], ("dom", "rep"))
    own_rows = pl.pallas_call(
        sum_kernel,
        out_shape=jax.ShapeDtypeStruct((share, width), f32),
        compiler_params=params(),
    )(parts)
    own_rows = lax.psum(own_rows, "rep")
    grad_nodes = pl.pallas_call(
        finish_kernel,
        out_shape=jax.ShapeDtypeStruct((n, width), bf16),
        compiler_params=params(),
    )(listed, returned, edge_in_w, base)
    return (grad_nodes[None], grad_edges[None], own_rows, vector_total)


def solution(mesh):
    in_specs = (
        P("rep", "dom", None),
        P("rep", "dom", None),
        P("rep", "dom", None),
        P("rep", "dom", None),
        P(),
        P(),
        P(),
        P(),
        P(),
        P(),
        P(),
        P(),
        P("dom"),
        P("dom"),
        P("dom", None),
        P("dom"),
    )
    out_specs = (P("rep", "dom", None), P("rep", "dom", None), P("dom", None), P())
    return jax.shard_map(shards, mesh=mesh, in_specs=in_specs, out_specs=out_specs, check_vma=False)
```

```python
import jax
import jax.numpy as jnp
from jax import lax
from jax.experimental import pallas as pl
from jax.experimental.pallas import tpu as pltpu
from jax.sharding import PartitionSpec as P

epsilon = 1e-05
f32 = jnp.float32
bf16 = jnp.bfloat16
NT = (((1,), (1,)), ((), ()))
TN = (((0,), (0,)), ((), ()))
VMEM_LIMIT = 58 * 1024 * 1024
CHUNK = 1024
DEAD = 0x10000


def mm(a, b):
    return jnp.dot(a, b, preferred_element_type=f32)


def mm_nt(a, b):
    return lax.dot_general(a, b, NT, preferred_element_type=f32)


def mm_tn(a, b):
    return lax.dot_general(a, b, TN, preferred_element_type=f32)


def params():
    return pltpu.CompilerParams(vmem_limit_bytes=VMEM_LIMIT)


def cost(flops, moved):
    return pl.CostEstimate(flops=flops, bytes_accessed=moved, transcendentals=0)


def one_hot_t(row, first, count):
    ids = lax.broadcasted_iota(jnp.int32, (count, row.shape[1]), 0) + first
    return jnp.where(ids == row, 1.0, 0.0).astype(bf16)


def columns(row):
    k = row.shape[1]
    parts = [
        jnp.transpose(jnp.broadcast_to(row[:, i : i + 128], (128, 128))) for i in range(0, k, 128)
    ]
    return jnp.concatenate(parts, axis=0)


def one_hot(column, first, count):
    lane = lax.broadcasted_iota(jnp.int32, column.shape, 1)
    parts = [
        jnp.where(column == lane + (first + i), 1.0, 0.0).astype(bf16)
        for i in range(0, count, 128)
    ]
    return jnp.concatenate(parts, axis=1)


def sigmoid(value):
    return 0.5 * jnp.tanh(0.5 * value) + 0.5


def normalise(value):
    center = value - jnp.mean(value, axis=-1, keepdims=True)
    recip = lax.rsqrt(jnp.mean(center * center, axis=-1, keepdims=True) + epsilon)
    return center * recip, recip


def norm_backward(upper, normed, recip):
    return recip * (
        upper
        - jnp.mean(upper, axis=-1, keepdims=True)
        - normed * jnp.mean(upper * normed, axis=-1, keepdims=True)
    )


def send_kernel(rows_ref, nodes_ref, out_ref):
    n = nodes_ref.shape[0]
    regions, cap = rows_ref.shape
    listed = jnp.transpose(rows_ref[...])
    lane = lax.broadcasted_iota(jnp.int32, (cap, n), 1)
    picks = jnp.concatenate(
        [jnp.where(listed[:, q : q + 1] == lane, 1.0, 0.0).astype(bf16) for q in range(regions)],
        axis=0,
    )
    out_ref[...] = mm(picks, nodes_ref[...]).astype(bf16)


def before_kernel(
    snd_ref,
    rcv_ref,
    edges_ref,
    nodes_ref,
    ein_ref,
    ebias_ref,
    part_ref,
    local_ref,
    far_ref,
    rcv_t_ref,
    rcv_n_ref,
    table_scr,
):
    n, width = nodes_ref.shape
    remote = far_ref.shape[1]
    c = pl.program_id(0)

    @pl.when(c == 0)
    def _():
        table_scr[...] = mm(nodes_ref[...], ein_ref[2 * width :, :]).astype(bf16)

    snd = columns(snd_ref[pl.ds(c, 1), :])
    row = rcv_ref[pl.ds(c, 1), :]
    rcv = columns(row)
    near = one_hot(jnp.bitwise_and(rcv, DEAD - 1), 0, n)
    local_ref[...] = mm(one_hot(snd, 0, n), nodes_ref[...]).astype(bf16)
    far_ref[...] = one_hot(snd, n, remote)
    rcv_t_ref[...] = one_hot_t(row, 0, n)
    rcv_n_ref[...] = one_hot(rcv, 0, n)
    part_ref[...] = (
        mm(edges_ref[...], ein_ref[:width, :]) + mm(near, table_scr[...]) + ebias_ref[...]
    )


def deal(core, mats_ref, vecs, mine_ref, send_ref):
    blocks = mine_ref.shape[0]
    regions = 2 * blocks
    share, width = mats_ref.shape[0] // regions, mats_ref.shape[1]
    tail = jnp.concatenate(
        [vec[:, j : j + 128] for vec in vecs for j in range(0, width, 128)], axis=0
    ).astype(bf16)
    for out_ref, parity in ((mine_ref, core), (send_ref, 1 - core)):
        for i in range(blocks):
            at = pl.multiple_of((2 * i + parity) * share, 16)
            rows = mats_ref[pl.ds(at, share), :]
            for j in range(width // 128):
                out_ref[i, j * share : (j + 1) * share] = rows[:, j * 128 : (j + 1) * 128]
            out_ref[i, width // 128 * share :] = tail


def main_kernel(
    place_ref,
    egain_ref,
    nbias_ref,
    ngain_ref,
    part_hbm,
    local_hbm,
    far_hbm,
    rcv_t_hbm,
    rcv_n_hbm,
    cot_hbm,
    edges_hbm,
    nodes_hbm,
    ncot_hbm,
    arrived_hbm,
    ein_hbm,
    eout_hbm,
    nin_hbm,
    nout_hbm,
    hg_hbm,
    base_hbm,
    mine_hbm,
    send_hbm,
    part_ref,
    local_ref,
    far_ref,
    rcv_t_ref,
    rcv_n_ref,
    cot_ref,
    edges_ref,
    nodes_ref,
    ncot_ref,
    arrived_ref,
    ws_ref,
    wr_ref,
    eout_ref,
    nin_ref,
    nout_ref,
    hg_ref,
    base_ref,
    mine_ref,
    send_ref,
    act_ref,
    slope_ref,
    normed_ref,
    recip_ref,
    mats_ref,
    chunk_sems,
    sems,
    out_sems,
):
    count, width = part_ref.shape
    n = nodes_ref.shape[0]
    chunk = min(CHUNK, count)
    n_chunks = count // chunk
    streams = [
        (far_hbm, far_ref),
        (local_hbm, local_ref),
        (part_hbm, part_ref),
        (rcv_n_hbm, rcv_n_ref),
        (cot_hbm, cot_ref),
        (edges_hbm, edges_ref),
    ]

    def stream(k, c):
        src, dst = streams[k]
        at = pl.ds(c * chunk, chunk)
        return pltpu.make_async_copy(src.at[at], dst.at[at], chunk_sems.at[k, c])

    singles = [
        (arrived_hbm, arrived_ref),
        (ein_hbm.at[pl.ds(width, width)], ws_ref),
        (eout_hbm, eout_ref),
        (rcv_t_hbm, rcv_t_ref),
        (nodes_hbm, nodes_ref),
        (nin_hbm, nin_ref),
        (nout_hbm, nout_ref),
        (ncot_hbm, ncot_ref),
        (ein_hbm.at[pl.ds(2 * width, width)], wr_ref),
    ]
    single = [pltpu.make_async_copy(src, dst, sems.at[k]) for k, (src, dst) in enumerate(singles)]
    stream(0, 0).start()
    single[0].start()
    stream(1, 0).start()
    single[1].start()
    stream(2, 0).start()
    single[2].start()
    single[3].start()
    for c in range(1, n_chunks):
        for k in range(3):
            stream(k, c).start()
    for k in range(4, 8):
        single[k].start()
    for c in range(n_chunks):
        for k in range(3, 6):
            stream(k, c).start()
    single[8].start()

    egain = egain_ref[...]
    for c in range(n_chunks):
        here = pl.ds(c * chunk, chunk)
        stream(0, c).wait()
        stream(1, c).wait()
        if c == 0:
            single[0].wait()
        picked = local_ref[here, :] + mm(far_ref[here, :], arrived_ref[...]).astype(bf16)
        local_ref[here, :] = picked
        stream(2, c).wait()
        if c == 0:
            single[1].wait()
        hidden = part_ref[here, :] + mm(picked, ws_ref[...])
        s = sigmoid(hidden)
        act = (hidden * s).astype(bf16)
        act_ref[here, :] = act
        slope_ref[here, :] = s * (1.0 + hidden * (1.0 - s))
        if c == 0:
            single[2].wait()
        normed, recip = normalise(mm(act, eout_ref[...]))
        normed_ref[here, :] = normed
        recip_ref[here, :] = recip
        message = (normed * egain).astype(bf16)
        if c == 0:
            single[3].wait()
        term = mm(rcv_t_ref[:, c * chunk : (c + 1) * chunk], message)
        agg = term if c == 0 else agg + term

    for k in range(4, 8):
        single[k].wait()
    nodes = nodes_ref[...]
    agg = agg.astype(bf16)
    hidden = mm(nodes, nin_ref[:width, :]) + mm(agg, nin_ref[width:, :]) + nbias_ref[...]
    s = sigmoid(hidden)
    act = (hidden * s).astype(bf16)
    normed, recip = normalise(mm(act, nout_ref[...]))
    upstream = ncot_ref[...].astype(f32)
    pre_grad = norm_backward(upstream * ngain_ref[...], normed, recip).astype(bf16)
    hidden_grad = (mm_nt(pre_grad, nout_ref[...]) * (s * (1.0 + hidden * (1.0 - s)))).astype(bf16)
    agg_grad = mm_nt(hidden_grad, nin_ref[width:, :]).astype(bf16)
    vecs = [
        None,
        None,
        jnp.sum(hidden_grad.astype(f32), axis=0, keepdims=True),
        jnp.sum(upstream * normed, axis=0, keepdims=True),
    ]

    for c in range(n_chunks):
        here = pl.ds(c * chunk, chunk)
        stream(3, c).wait()
        picks = rcv_n_ref[here, :]
        live = jnp.max(picks.astype(f32), axis=1, keepdims=True) > 0.5
        gathered = mm(picks, agg_grad)
        stream(4, c).wait()
        message_grad = jnp.where(live, cot_ref[here, :].astype(f32) + gathered, 0.0)
        edge_normed = normed_ref[here, :]
        term = jnp.sum(message_grad * edge_normed, axis=0, keepdims=True)
        vecs[1] = term if c == 0 else vecs[1] + term
        edge_pre_grad = norm_backward(
            message_grad * egain, edge_normed, recip_ref[here, :]
        ).astype(bf16)
        edge_grad = (mm_nt(edge_pre_grad, eout_ref[...]) * slope_ref[here, :]).astype(bf16)
        hg_ref[here, :] = edge_grad
        pltpu.make_async_copy(hg_ref.at[here], hg_hbm.at[here], out_sems.at[c]).start()
        term = jnp.sum(edge_grad.astype(f32), axis=0, keepdims=True)
        vecs[0] = term if c == 0 else vecs[0] + term
        stream(5, c).wait()
        terms = [
            mm_tn(edges_ref[here, :], edge_grad),
            mm_tn(local_ref[here, :], edge_grad),
            mm_tn(act_ref[here, :], edge_pre_grad),
            mm(rcv_t_ref[:, c * chunk : (c + 1) * chunk], edge_grad),
        ]
        sums = terms if c == 0 else [a + b for a, b in zip(sums, terms)]

    single[8].wait()
    received = sums[3].astype(bf16)
    base_ref[...] = (
        upstream + mm_nt(hidden_grad, nin_ref[:width, :]) + mm_nt(received, wr_ref[...])
    )
    base_copy = pltpu.make_async_copy(base_ref, base_hbm, out_sems.at[n_chunks])
    base_copy.start()
    mats_ref[:width, :] = sums[0].astype(bf16)
    mats_ref[width : 2 * width, :] = sums[1].astype(bf16)
    mats_ref[2 * width : 3 * width, :] = mm_tn(nodes, received).astype(bf16)
    mats_ref[3 * width : 4 * width, :] = sums[2].astype(bf16)
    mats_ref[4 * width : 5 * width, :] = mm_tn(nodes, hidden_grad).astype(bf16)
    mats_ref[5 * width : 6 * width, :] = mm_tn(agg, hidden_grad).astype(bf16)
    mats_ref[6 * width :, :] = mm_tn(act, pre_grad).astype(bf16)
    deal(place_ref[0], mats_ref, vecs, mine_ref, send_ref)
    last = [
        pltpu.make_async_copy(send_ref, send_hbm, out_sems.at[n_chunks + 1]),
        pltpu.make_async_copy(mine_ref, mine_hbm, out_sems.at[n_chunks + 2]),
    ]
    for copy in last:
        copy.start()
    for c in range(n_chunks):
        here = pl.ds(c * chunk, chunk)
        pltpu.make_async_copy(hg_ref.at[here], hg_hbm.at[here], out_sems.at[c]).wait()
    base_copy.wait()
    for copy in last:
        copy.wait()


def senders_kernel(snd_ref, hg_ref, ws_ref, base_ref, sent_ref, out_ref):
    n, width = base_ref.shape
    remote = sent_ref.shape[0]
    snd = snd_ref[...]
    local = mm(one_hot_t(snd, 0, n), hg_ref[...]).astype(bf16)
    out_ref[...] = base_ref[...] + mm_nt(local, ws_ref[...])
    tile = 256 if remote % 256 == 0 else remote

    @pl.loop(0, remote // tile)
    def _(i):
        at = pl.multiple_of(i * tile, tile)
        part = mm(one_hot_t(snd, n + at, tile), hg_ref[...]).astype(bf16)
        sent_ref[pl.ds(at, tile), :] = part


def edges_kernel(hg_ref, cot_ref, w_ref, out_ref):
    out_ref[...] = (cot_ref[...].astype(f32) + mm_nt(hg_ref[...], w_ref[...])).astype(bf16)


def finish_kernel(rows_ref, returned_ref, ws_ref, base_ref, out_ref):
    n, width = base_ref.shape
    own = mm(one_hot_t(rows_ref[...], 0, n), returned_ref[...]).astype(bf16)
    out_ref[...] = (base_ref[...] + mm_nt(own, ws_ref[...])).astype(bf16)


def over_chips_kernel(parts_ref, own_ref, sent_ref):
    total = jnp.sum(parts_ref[...].astype(f32), axis=0)
    own_ref[...] = total
    sent_ref[...] = total.astype(bf16)


def join_kernel(*refs):
    mats_ref, vecs_ref = refs[-2:]
    share, width = mats_ref.shape
    total = refs[0][...]
    for ref in refs[1:-2]:
        total = total + ref[...].astype(f32)
    slabs = width // 128
    for j in range(slabs):
        mats_ref[:, j * 128 : (j + 1) * 128] = total[j * share : (j + 1) * share]
        for k in range(4):
            at = slabs * share + k * slabs + j
            vecs_ref[k : k + 1, j * 128 : (j + 1) * 128] = total[at : at + 1]


def shards(
    node_feat,
    edge_feat,
    node_cot,
    edge_cot,
    edge_in_w,
    edge_bias,
    edge_out_w,
    edge_gain,
    node_in_w,
    node_bias,
    node_out_w,
    node_gain,
    senders,
    receivers,
    send_rows,
    live_edges,
):
    nodes = node_feat[0]
    edges = edge_feat[0]
    cots = edge_cot[0]
    n, width = nodes.shape
    count = edges.shape[0]
    regions, cap = send_rows.shape
    remote = regions * cap
    chunk = min(CHUNK, count)
    n_chunks = count // chunk
    rows = edge_in_w.shape[0] + edge_out_w.shape[0] + node_in_w.shape[0] + node_out_w.shape[0]
    share = rows // regions
    chips = regions // 2
    reps = lax.axis_size("rep")
    core = lax.rem(lax.axis_index("dom"), 2).reshape(1)
    smem = pl.BlockSpec(memory_space=pltpu.SMEM)
    vmem = pl.BlockSpec(memory_space=pltpu.VMEM)
    shape = jax.ShapeDtypeStruct

    def whole(shape):
        return pl.BlockSpec(shape, lambda i: (0,) * len(shape))

    def rows_of(width):
        return pl.BlockSpec((chunk, width), lambda i: (i, 0))

    outgoing = pl.pallas_call(
        send_kernel,
        out_shape=shape((remote, width), bf16),
        compiler_params=params(),
        cost_estimate=cost(2 * remote * n * width, 4 * remote * width),
    )(send_rows, nodes)
    arrived = lax.all_to_all(
        outgoing.reshape(regions, cap, width), "dom", split_axis=0, concat_axis=0, tiled=True
    ).reshape(remote, width)

    live = jnp.arange(count, dtype=jnp.int32) < live_edges[0]
    rcv = jnp.where(live, receivers, receivers + DEAD).reshape(n_chunks, chunk)
    hidden_part, local, far, rcv_t, rcv_n = pl.pallas_call(
        before_kernel,
        grid=(n_chunks,),
        in_specs=[
            whole((n_chunks, chunk)),
            whole((n_chunks, chunk)),
            rows_of(width),
            whole((n, width)),
            whole(edge_in_w.shape),
            whole((1, width)),
        ],
        out_specs=[
            rows_of(width),
            rows_of(width),
            rows_of(remote),
            pl.BlockSpec((n, chunk), lambda i: (0, i)),
            rows_of(n),
        ],
        out_shape=[
            shape((count, width), f32),
            shape((count, width), bf16),
            shape((count, remote), bf16),
            shape((n, count), bf16),
            shape((count, n), bf16),
        ],
        scratch_shapes=[pltpu.VMEM((n, width), bf16)],
        compiler_params=params(),
        cost_estimate=cost(6_000_000_000, 16_000_000),
    )(
        senders.reshape(n_chunks, chunk),
        rcv,
        edges,
        nodes,
        edge_in_w,
        edge_bias.reshape(1, width),
    )

    hbm = pl.BlockSpec(memory_space=pl.ANY)
    slab = (share * width + 4 * width) // 128
    dealt = (chips, slab, 128)
    hidden_grad, base, mine, to_other = pl.pallas_call(
        main_kernel,
        in_specs=[smem, vmem, vmem, vmem] + [hbm] * 14,
        out_specs=[hbm] * 4,
        out_shape=[
            shape((count, width), bf16),
            shape((n, width), f32),
            shape(dealt, bf16),
            shape(dealt, bf16),
        ],
        scratch_shapes=[
            pltpu.VMEM((count, width), f32),
            pltpu.VMEM((count, width), bf16),
            pltpu.VMEM((count, remote), bf16),
            pltpu.VMEM((n, count), bf16),
            pltpu.VMEM((count, n), bf16),
            pltpu.VMEM((count, width), bf16),
            pltpu.VMEM((count, width), bf16),
            pltpu.VMEM((n, width), bf16),
            pltpu.VMEM((n, width), bf16),
            pltpu.VMEM((remote, width), bf16),
            pltpu.VMEM((width, width), bf16),
            pltpu.VMEM((width, width), bf16),
            pltpu.VMEM(edge_out_w.shape, bf16),
            pltpu.VMEM(node_in_w.shape, bf16),
            pltpu.VMEM(node_out_w.shape, bf16),
            pltpu.VMEM((count, width), bf16),
            pltpu.VMEM((n, width), f32),
            pltpu.VMEM(dealt, bf16),
            pltpu.VMEM(dealt, bf16),
            pltpu.VMEM((count, width), bf16),
            pltpu.VMEM((count, width), f32),
            pltpu.VMEM((count, width), f32),
            pltpu.VMEM((count, 1), f32),
            pltpu.VMEM((rows, width), bf16),
            pltpu.SemaphoreType.DMA((6, n_chunks)),
            pltpu.SemaphoreType.DMA((9,)),
            pltpu.SemaphoreType.DMA((n_chunks + 3,)),
        ],
        compiler_params=params(),
        cost_estimate=cost(16_000_000_000, 30_000_000),
    )(
        core,
        edge_gain.reshape(1, width),
        node_bias.reshape(1, width),
        node_gain.reshape(1, width),
        hidden_part,
        local,
        far,
        rcv_t,
        rcv_n,
        cots,
        edges,
        nodes,
        node_cot[0],
        arrived,
        edge_in_w,
        edge_out_w,
        node_in_w,
        node_out_w,
    )

    one_block = pl.BlockSpec((width, width), lambda i: (1, 0))
    from_other = lax.ppermute(to_other, "dom", [(i, i ^ 1) for i in range(regions)])
    chip_sum = (mine.astype(f32) + from_other.astype(f32)).astype(bf16)
    chip_sum, hidden_grad = lax.optimization_barrier((chip_sum, hidden_grad))
    by_chip = lax.all_to_all(
        chip_sum,
        "dom",
        split_axis=0,
        concat_axis=0,
        axis_index_groups=[list(range(c, regions, 2)) for c in range(2)],
        tiled=True,
    )
    sent, base = pl.pallas_call(
        senders_kernel,
        grid=(1,),
        in_specs=[vmem, vmem, one_block, vmem],
        out_shape=(shape((remote, width), bf16), shape((n, width), f32)),
        compiler_params=params(),
        cost_estimate=cost(1000, 1000),
    )(senders.reshape(1, count), hidden_grad, edge_in_w, base)
    grad_edges = pl.pallas_call(
        edges_kernel,
        grid=(n_chunks,),
        in_specs=[
            rows_of(width),
            rows_of(width),
            pl.BlockSpec((width, width), lambda i: (0, 0)),
        ],
        out_specs=rows_of(width),
        out_shape=shape((count, width), bf16),
        compiler_params=params(),
        cost_estimate=cost(1000, 1000),
    )(hidden_grad, cots, edge_in_w)

    by_chip, sent, grad_edges = lax.optimization_barrier((by_chip, sent, grad_edges))
    returned = lax.all_to_all(
        sent.reshape(regions, cap, width), "dom", split_axis=0, concat_axis=0, tiled=True
    ).reshape(remote, width)
    total, total_bf16 = pl.pallas_call(
        over_chips_kernel,
        out_shape=(shape((slab, 128), f32), shape((slab, 128), bf16)),
        compiler_params=params(),
        cost_estimate=cost(1_000_000, 2_000_000),
    )(by_chip)
    totals = [total] + [
        lax.ppermute(total_bf16, "rep", [(i, (i + k) % reps) for i in range(reps)])
        for k in range(1, reps)
    ]
    grad_nodes = pl.pallas_call(
        finish_kernel,
        grid=(1,),
        in_specs=[vmem, vmem, one_block, vmem],
        out_shape=shape((n, width), bf16),
        compiler_params=params(),
        cost_estimate=cost(1000, 1000),
    )(send_rows.reshape(1, remote), returned, edge_in_w, base)
    own_rows, vector_total = pl.pallas_call(
        join_kernel,
        out_shape=(shape((share, width), f32), shape((4, width), f32)),
        compiler_params=params(),
    )(*totals)
    return (grad_nodes[None], grad_edges[None], own_rows, vector_total)


def solution(mesh):
    in_specs = (
        P("rep", "dom", None),
        P("rep", "dom", None),
        P("rep", "dom", None),
        P("rep", "dom", None),
        P(),
        P(),
        P(),
        P(),
        P(),
        P(),
        P(),
        P(),
        P("dom"),
        P("dom"),
        P("dom", None),
        P("dom"),
    )
    out_specs = (P("rep", "dom", None), P("rep", "dom", None), P("dom", None), P())
    return jax.shard_map(shards, mesh=mesh, in_specs=in_specs, out_specs=out_specs, check_vma=False)
```

```python
import jax
import jax.numpy as jnp
from jax import lax
from jax.experimental import pallas as pl
from jax.experimental.pallas import tpu as pltpu
from jax.sharding import PartitionSpec as P

epsilon = 1e-05
f32 = jnp.float32
bf16 = jnp.bfloat16
NT = (((1,), (1,)), ((), ()))
TN = (((0,), (0,)), ((), ()))
MAIN_LIMIT = 50
BEFORE_LIMIT = 60
CHUNK = 1024
PART = bf16
KEPT = bf16


def mm(a, b):
    return jnp.dot(a, b, preferred_element_type=f32)


def mm_nt(a, b):
    return lax.dot_general(a, b, NT, preferred_element_type=f32)


def mm_tn(a, b):
    return lax.dot_general(a, b, TN, preferred_element_type=f32)


def params(limit=16):
    return pltpu.CompilerParams(vmem_limit_bytes=limit * 1024 * 1024)


def cost(flops, moved):
    return pl.CostEstimate(flops=flops, bytes_accessed=moved, transcendentals=0)


def one_hot_t(row, first, count):
    ids = lax.broadcasted_iota(jnp.int32, (count, row.shape[1]), 0) + first
    return jnp.where(ids == row, 1.0, 0.0).astype(bf16)


def columns(row):
    k = row.shape[1]
    parts = [
        jnp.transpose(jnp.broadcast_to(row[:, i : i + 128], (128, 128))) for i in range(0, k, 128)
    ]
    return jnp.concatenate(parts, axis=0)


def one_hot(column, first, count):
    lane = lax.broadcasted_iota(jnp.int32, column.shape, 1)
    parts = [
        jnp.where(column == lane + (first + i), 1.0, 0.0).astype(bf16)
        for i in range(0, count, 128)
    ]
    return jnp.concatenate(parts, axis=1)


def sigmoid(value):
    return 0.5 * jnp.tanh(0.5 * value) + 0.5


def normalise(value, live=None):
    center = value - jnp.mean(value, axis=-1, keepdims=True)
    recip = lax.rsqrt(jnp.mean(center * center, axis=-1, keepdims=True) + epsilon)
    if live is not None:
        recip = jnp.where(live, recip, 0.0)
    return center * recip, recip


def norm_backward(upper, normed, recip):
    return recip * (
        upper
        - jnp.mean(upper, axis=-1, keepdims=True)
        - normed * jnp.mean(upper * normed, axis=-1, keepdims=True)
    )


def send_kernel(rows_ref, nodes_ref, out_hbm, out_ref, sems):
    n = nodes_ref.shape[0]
    regions, cap = rows_ref.shape
    listed = jnp.transpose(rows_ref[...])
    lane = lax.broadcasted_iota(jnp.int32, (cap, n), 1)
    pieces = sems.shape[0]
    group = regions // pieces
    copies = []
    for p in range(pieces):
        picks = jnp.concatenate(
            [
                jnp.where(listed[:, q : q + 1] == lane, 1.0, 0.0).astype(bf16)
                for q in range(p * group, (p + 1) * group)
            ],
            axis=0,
        )
        at = pl.ds(p * group * cap, group * cap)
        out_ref[at, :] = mm(picks, nodes_ref[...]).astype(bf16)
        copies.append(pltpu.make_async_copy(out_ref.at[at], out_hbm.at[at], sems.at[p]))
        copies[-1].start()
    for copy in copies:
        copy.wait()


def before_kernel(
    snd_ref,
    rcv_ref,
    edges_ref,
    nodes_ref,
    ein_ref,
    ebias_ref,
    part_ref,
    local_ref,
    far_ref,
    rcv_n_ref,
    table_scr,
):
    n, width = nodes_ref.shape
    remote = far_ref.shape[1]
    c = pl.program_id(0)

    @pl.when(c == 0)
    def _():
        table_scr[...] = mm(nodes_ref[...], ein_ref[2 * width :, :]).astype(bf16)

    snd = columns(snd_ref[pl.ds(c, 1), :])
    near = one_hot(columns(rcv_ref[pl.ds(c, 1), :]), 0, n)
    rcv_n_ref[...] = near
    local_ref[...] = mm(one_hot(snd, 0, n), nodes_ref[...]).astype(bf16)
    far_ref[...] = one_hot(snd, n, remote)
    part_ref[...] = (
        mm(edges_ref[...], ein_ref[:width, :]) + mm(near, table_scr[...]) + ebias_ref[...]
    ).astype(part_ref.dtype)


def deal(core, mats_ref, vecs, mine_ref, send_ref):
    blocks = mine_ref.shape[0]
    regions = 2 * blocks
    share, width = mats_ref.shape[0] // regions, mats_ref.shape[1]
    tail = jnp.concatenate(
        [vec[:, j : j + 128] for vec in vecs for j in range(0, width, 128)], axis=0
    ).astype(bf16)
    for out_ref, parity in ((mine_ref, core), (send_ref, 1 - core)):
        for i in range(blocks):
            at = pl.multiple_of((2 * i + parity) * share, 16)
            rows = mats_ref[pl.ds(at, share), :]
            for j in range(width // 128):
                out_ref[i, j * share : (j + 1) * share] = rows[:, j * 128 : (j + 1) * 128]
            out_ref[i, width // 128 * share :] = tail


def main_kernel(
    place_ref,
    live_ref,
    egain_ref,
    nbias_ref,
    ngain_ref,
    arrived_ref,
    part_hbm,
    local_hbm,
    far_hbm,
    rcv_n_hbm,
    cot_hbm,
    edges_hbm,
    nodes_hbm,
    ncot_hbm,
    ein_hbm,
    eout_hbm,
    nin_hbm,
    nout_hbm,
    hg_ref,
    base_ref,
    mine_ref,
    send_ref,
    part_ref,
    far_ref,
    x_ref,
    cot_ref,
    node_in_ref,
    ncot_ref,
    ws_ref,
    wr_ref,
    eout_ref,
    nin_ref,
    nout_ref,
    act_ref,
    slope_ref,
    normed_ref,
    recip_ref,
    mats_ref,
    pg_ref,
    chunk_sems,
    sems,
):
    count, width = part_ref.shape
    n = ncot_ref.shape[0]
    chunk = min(CHUNK, count)
    n_chunks = count // chunk
    streams = [
        (far_hbm, far_ref),
        (local_hbm, x_ref.at[:, pl.ds(width, width)]),
        (part_hbm, part_ref),
        (rcv_n_hbm, x_ref.at[:, pl.ds(2 * width, n)]),
        (cot_hbm, cot_ref),
        (edges_hbm, x_ref.at[:, pl.ds(0, width)]),
    ]

    def stream(k, c):
        src, dst = streams[k]
        at = pl.ds(c * chunk, chunk)
        return pltpu.make_async_copy(src.at[at], dst.at[at], chunk_sems.at[k, c])

    singles = [
        (ein_hbm.at[pl.ds(width, width)], ws_ref),
        (eout_hbm, eout_ref),
        (nodes_hbm, node_in_ref.at[:, pl.ds(0, width)]),
        (nin_hbm, nin_ref),
        (nout_hbm, nout_ref),
        (ncot_hbm, ncot_ref),
        (ein_hbm.at[pl.ds(2 * width, width)], wr_ref),
    ]
    single = [pltpu.make_async_copy(src, dst, sems.at[k]) for k, (src, dst) in enumerate(singles)]
    stream(0, 0).start()
    stream(1, 0).start()
    single[0].start()
    stream(2, 0).start()
    single[1].start()
    for c in range(1, n_chunks):
        for k in range(3):
            stream(k, c).start()
    for c in range(n_chunks):
        stream(3, c).start()
    for k in range(2, 6):
        single[k].start()
    for c in range(n_chunks):
        for k in range(4, 6):
            stream(k, c).start()
    single[6].start()

    egain = egain_ref[...]

    def rows_at(c):
        return pl.ds(c * chunk, chunk)

    def pick(c):
        here = rows_at(c)
        x_ref[here, width : 2 * width] += mm(far_ref[here, :], arrived_ref[...]).astype(bf16)

    def activate(c):
        here = rows_at(c)
        hidden = part_ref[here, :] + mm(x_ref[here, width : 2 * width], ws_ref[...])
        s = sigmoid(hidden)
        act_ref[here, :] = (hidden * s).astype(bf16)
        slope_ref[here, :] = (s * (1.0 + hidden * (1.0 - s))).astype(KEPT)

    def send_message(c):
        here = rows_at(c)
        live = lax.broadcasted_iota(jnp.int32, (chunk, 1), 0) + c * chunk < live_ref[0]
        normed, recip = normalise(mm(act_ref[here, :], eout_ref[...]), live)
        normed_ref[here, :] = normed.astype(KEPT)
        recip_ref[here, :] = recip
        pg_ref[here, :] = (normed * egain).astype(bf16)

    def skewed(stages, before):
        for t in range(n_chunks + len(stages) - 1):
            for k in range(len(stages)):
                if 0 <= t - k < n_chunks:
                    before[k](t - k)
            for k in reversed(range(len(stages))):
                if 0 <= t - k < n_chunks:
                    stages[k](t - k)

    def nothing(c):
        pass

    def wait_pick(c):
        stream(0, c).wait()
        stream(1, c).wait()

    def wait_activate(c):
        stream(2, c).wait()
        if c == 0:
            single[0].wait()

    def wait_message(c):
        if c == 0:
            single[1].wait()

    skewed([pick, activate, send_message], [wait_pick, wait_activate, wait_message])
    for c in range(n_chunks):
        stream(3, c).wait()
    agg = mm_tn(x_ref[:, 2 * width :], pg_ref[...])

    for k in range(2, 6):
        single[k].wait()
    node_in_ref[:, width:] = agg.astype(bf16)
    node_in = node_in_ref[...]
    nodes = node_in_ref[:, :width]
    hidden = mm(node_in, nin_ref[...]) + nbias_ref[...]
    s = sigmoid(hidden)
    act = (hidden * s).astype(bf16)
    normed, recip = normalise(mm(act, nout_ref[...]))
    upstream = ncot_ref[...].astype(f32)
    pre_grad = norm_backward(upstream * ngain_ref[...], normed, recip).astype(bf16)
    hidden_grad = (mm_nt(pre_grad, nout_ref[...]) * (s * (1.0 + hidden * (1.0 - s)))).astype(bf16)
    node_in_grad = mm_nt(hidden_grad, nin_ref[...])
    agg_grad = node_in_grad[:, width:].astype(bf16)
    vecs = [
        None,
        None,
        jnp.sum(hidden_grad.astype(f32), axis=0, keepdims=True),
        jnp.sum(upstream * normed, axis=0, keepdims=True),
    ]

    def take_gradient(c):
        here = rows_at(c)
        message_grad = cot_ref[here, :].astype(f32) + mm(x_ref[here, 2 * width :], agg_grad)
        edge_normed = normed_ref[here, :].astype(f32)
        term = jnp.sum(message_grad * edge_normed, axis=0, keepdims=True)
        vecs[1] = term if c == 0 else vecs[1] + term
        pg_ref[here, :] = norm_backward(
            message_grad * egain, edge_normed, recip_ref[here, :]
        ).astype(bf16)

    def pass_gradient(c):
        here = rows_at(c)
        edge_grad = (mm_nt(pg_ref[here, :], eout_ref[...]) * slope_ref[here, :].astype(f32)).astype(bf16)
        hg_ref[here, :] = edge_grad
        term = jnp.sum(edge_grad.astype(f32), axis=0, keepdims=True)
        vecs[0] = term if c == 0 else vecs[0] + term

    def wait_take(c):
        stream(4, c).wait()

    skewed([take_gradient, pass_gradient], [wait_take, nothing])
    for c in range(n_chunks):
        stream(5, c).wait()
    by_inputs = mm_tn(x_ref[...], hg_ref[...])

    single[6].wait()
    received = by_inputs[2 * width :].astype(bf16)
    base_ref[...] = (
        upstream + node_in_grad[:, :width] + mm_nt(received, wr_ref[...])
    )
    mats_ref[: 2 * width, :] = by_inputs[: 2 * width].astype(bf16)
    mats_ref[2 * width : 3 * width, :] = mm_tn(nodes, received).astype(bf16)
    mats_ref[3 * width : 4 * width, :] = mm_tn(act_ref[...], pg_ref[...]).astype(bf16)
    mats_ref[4 * width : 6 * width, :] = mm_tn(node_in, hidden_grad).astype(bf16)
    mats_ref[6 * width :, :] = mm_tn(act, pre_grad).astype(bf16)
    deal(place_ref[0], mats_ref, vecs, mine_ref, send_ref)


def senders_kernel(snd_ref, hg_ref, ws_ref, base_ref, sent_ref, out_ref):
    n, width = base_ref.shape
    remote = sent_ref.shape[0]
    snd = snd_ref[...]
    local = mm(one_hot_t(snd, 0, n), hg_ref[...]).astype(bf16)
    out_ref[...] = base_ref[...] + mm_nt(local, ws_ref[...])
    tile = 256 if remote % 256 == 0 else remote

    @pl.loop(0, remote // tile)
    def _(i):
        at = pl.multiple_of(i * tile, tile)
        part = mm(one_hot_t(snd, n + at, tile), hg_ref[...]).astype(bf16)
        sent_ref[pl.ds(at, tile), :] = part


def edges_kernel(hg_ref, cot_ref, w_ref, out_ref):
    out_ref[...] = (cot_ref[...].astype(f32) + mm_nt(hg_ref[...], w_ref[...])).astype(bf16)


def finish_kernel(rows_ref, returned_ref, ws_ref, base_ref, out_ref):
    n, width = base_ref.shape
    own = mm(one_hot_t(rows_ref[...], 0, n), returned_ref[...]).astype(bf16)
    out_ref[...] = (base_ref[...] + mm_nt(own, ws_ref[...])).astype(bf16)


def over_chips_kernel(parts_ref, own_ref, sent_ref):
    total = jnp.sum(parts_ref[...].astype(f32), axis=0)
    own_ref[...] = total
    sent_ref[...] = total.astype(bf16)


def join_kernel(*refs):
    mats_ref, vecs_ref = refs[-2:]
    share, width = mats_ref.shape
    total = refs[0][...]
    for ref in refs[1:-2]:
        total = total + ref[...].astype(f32)
    slabs = width // 128
    for j in range(slabs):
        mats_ref[:, j * 128 : (j + 1) * 128] = total[j * share : (j + 1) * share]
        for k in range(4):
            at = slabs * share + k * slabs + j
            vecs_ref[k : k + 1, j * 128 : (j + 1) * 128] = total[at : at + 1]


def shards(
    node_feat,
    edge_feat,
    node_cot,
    edge_cot,
    edge_in_w,
    edge_bias,
    edge_out_w,
    edge_gain,
    node_in_w,
    node_bias,
    node_out_w,
    node_gain,
    senders,
    receivers,
    send_rows,
    live_edges,
):
    nodes = node_feat[0]
    edges = edge_feat[0]
    cots = edge_cot[0]
    n, width = nodes.shape
    count = edges.shape[0]
    regions, cap = send_rows.shape
    remote = regions * cap
    chunk = min(CHUNK, count)
    n_chunks = count // chunk
    rows = edge_in_w.shape[0] + edge_out_w.shape[0] + node_in_w.shape[0] + node_out_w.shape[0]
    share = rows // regions
    chips = regions // 2
    reps = lax.axis_size("rep")
    core = lax.rem(lax.axis_index("dom"), 2).reshape(1)
    smem = pl.BlockSpec(memory_space=pltpu.SMEM)
    vmem = pl.BlockSpec(memory_space=pltpu.VMEM)
    hbm = pl.BlockSpec(memory_space=pl.ANY)
    shape = jax.ShapeDtypeStruct

    def whole(shape):
        return pl.BlockSpec(shape, lambda i: (0,) * len(shape))

    def rows_of(width):
        return pl.BlockSpec((chunk, width), lambda i: (i, 0))

    outgoing = pl.pallas_call(
        send_kernel,
        out_specs=hbm,
        out_shape=shape((remote, width), bf16),
        scratch_shapes=[
            pltpu.VMEM((remote, width), bf16),
            pltpu.SemaphoreType.DMA((4,)),
        ],
        compiler_params=params(58),
        cost_estimate=cost(2 * remote * n * width, 4 * remote * width),
    )(send_rows, nodes)
    arrived = lax.all_to_all(
        outgoing.reshape(regions, cap, width), "dom", split_axis=0, concat_axis=0, tiled=True
    ).reshape(remote, width)

    hidden_part, local, far, rcv_n = pl.pallas_call(
        before_kernel,
        grid=(n_chunks,),
        in_specs=[
            whole((n_chunks, chunk)),
            whole((n_chunks, chunk)),
            rows_of(width),
            whole((n, width)),
            whole(edge_in_w.shape),
            whole((1, width)),
        ],
        out_specs=[
            rows_of(width),
            rows_of(width),
            rows_of(remote),
            rows_of(n),
        ],
        out_shape=[
            shape((count, width), PART),
            shape((count, width), bf16),
            shape((count, remote), bf16),
            shape((count, n), bf16),
        ],
        scratch_shapes=[pltpu.VMEM((n, width), bf16)],
        compiler_params=params(BEFORE_LIMIT),
        cost_estimate=cost(6_000_000_000, 16_000_000),
    )(
        senders.reshape(n_chunks, chunk),
        receivers.reshape(n_chunks, chunk),
        edges,
        nodes,
        edge_in_w,
        edge_bias.reshape(1, width),
    )

    slab = (share * width + 4 * width) // 128
    dealt = (chips, slab, 128)
    hidden_grad, base, mine, to_other = pl.pallas_call(
        main_kernel,
        in_specs=[smem] * 2 + [vmem] * 4 + [hbm] * 12,
        out_specs=[vmem] * 4,
        out_shape=[
            shape((count, width), bf16),
            shape((n, width), f32),
            shape(dealt, bf16),
            shape(dealt, bf16),
        ],
        scratch_shapes=[
            pltpu.VMEM((count, width), PART),
            pltpu.VMEM((count, remote), bf16),
            pltpu.VMEM((count, 2 * width + n), bf16),
            pltpu.VMEM((count, width), bf16),
            pltpu.VMEM((n, 2 * width), bf16),
            pltpu.VMEM((n, width), bf16),
            pltpu.VMEM((width, width), bf16),
            pltpu.VMEM((width, width), bf16),
            pltpu.VMEM(edge_out_w.shape, bf16),
            pltpu.VMEM(node_in_w.shape, bf16),
            pltpu.VMEM(node_out_w.shape, bf16),
            pltpu.VMEM((count, width), bf16),
            pltpu.VMEM((count, width), KEPT),
            pltpu.VMEM((count, width), KEPT),
            pltpu.VMEM((count, 1), f32),
            pltpu.VMEM((rows, width), bf16),
            pltpu.VMEM((count, width), bf16),
            pltpu.SemaphoreType.DMA((6, n_chunks)),
            pltpu.SemaphoreType.DMA((7,)),
        ],
        compiler_params=params(MAIN_LIMIT),
        cost_estimate=cost(16_000_000_000, 30_000_000),
    )(
        core,
        live_edges,
        edge_gain.reshape(1, width),
        node_bias.reshape(1, width),
        node_gain.reshape(1, width),
        arrived,
        hidden_part,
        local,
        far,
        rcv_n,
        cots,
        edges,
        nodes,
        node_cot[0],
        edge_in_w,
        edge_out_w,
        node_in_w,
        node_out_w,
    )

    w_s = edge_in_w[width : 2 * width]
    from_other = lax.ppermute(to_other, "dom", [(i, i ^ 1) for i in range(regions)])
    chip_sum = (mine.astype(f32) + from_other.astype(f32)).astype(bf16)
    chip_sum, hidden_grad = lax.optimization_barrier((chip_sum, hidden_grad))
    by_chip = lax.all_to_all(
        chip_sum,
        "dom",
        split_axis=0,
        concat_axis=0,
        axis_index_groups=[list(range(c, regions, 2)) for c in range(2)],
        tiled=True,
    )
    sent, base = pl.pallas_call(
        senders_kernel,
        out_shape=(shape((remote, width), bf16), shape((n, width), f32)),
        compiler_params=params(),
        cost_estimate=cost(1000, 1000),
    )(senders.reshape(1, count), hidden_grad, w_s, base)
    grad_edges = pl.pallas_call(
        edges_kernel,
        grid=(n_chunks,),
        in_specs=[
            rows_of(width),
            rows_of(width),
            pl.BlockSpec((width, width), lambda i: (0, 0)),
        ],
        out_specs=rows_of(width),
        out_shape=shape((count, width), bf16),
        compiler_params=params(),
        cost_estimate=cost(1000, 1000),
    )(hidden_grad, cots, edge_in_w)

    by_chip, sent, grad_edges = lax.optimization_barrier((by_chip, sent, grad_edges))
    returned = lax.all_to_all(
        sent.reshape(regions, cap, width), "dom", split_axis=0, concat_axis=0, tiled=True
    ).reshape(remote, width)
    total, total_bf16 = pl.pallas_call(
        over_chips_kernel,
        out_shape=(shape((slab, 128), f32), shape((slab, 128), bf16)),
        compiler_params=params(),
        cost_estimate=cost(1_000_000, 2_000_000),
    )(by_chip)
    totals = [total] + [
        lax.ppermute(total_bf16, "rep", [(i, (i + k) % reps) for i in range(reps)])
        for k in range(1, reps)
    ]
    grad_nodes = pl.pallas_call(
        finish_kernel,
        out_shape=shape((n, width), bf16),
        compiler_params=params(),
        cost_estimate=cost(1000, 1000),
    )(send_rows.reshape(1, remote), returned, w_s, base)
    own_rows, vector_total = pl.pallas_call(
        join_kernel,
        out_shape=(shape((share, width), f32), shape((4, width), f32)),
        compiler_params=params(),
    )(*totals)
    return (grad_nodes[None], grad_edges[None], own_rows, vector_total)


def solution(mesh):
    in_specs = (
        P("rep", "dom", None),
        P("rep", "dom", None),
        P("rep", "dom", None),
        P("rep", "dom", None),
        P(),
        P(),
        P(),
        P(),
        P(),
        P(),
        P(),
        P(),
        P("dom"),
        P("dom"),
        P("dom", None),
        P("dom"),
    )
    out_specs = (P("rep", "dom", None), P("rep", "dom", None), P("dom", None), P())
    return jax.shard_map(shards, mesh=mesh, in_specs=in_specs, out_specs=out_specs, check_vma=False)
```

```python
import jax
import jax.numpy as jnp
from jax import lax
from jax.experimental import pallas as pl
from jax.experimental.pallas import tpu as pltpu
from jax.sharding import PartitionSpec as P

epsilon = 1e-05
f32 = jnp.float32
bf16 = jnp.bfloat16
NT = (((1,), (1,)), ((), ()))
TN = (((0,), (0,)), ((), ()))
MAIN_LIMIT = 48
BEFORE_LIMIT = 60
CHUNK = 1024
KEPT = bf16


def mm(a, b):
    return jnp.dot(a, b, preferred_element_type=f32)


def mm_nt(a, b):
    return lax.dot_general(a, b, NT, preferred_element_type=f32)


def mm_tn(a, b):
    return lax.dot_general(a, b, TN, preferred_element_type=f32)


def params(limit=16):
    return pltpu.CompilerParams(vmem_limit_bytes=limit * 1024 * 1024)


def cost(flops, moved):
    return pl.CostEstimate(flops=flops, bytes_accessed=moved, transcendentals=0)


def one_hot_t(row, first, count):
    ids = lax.broadcasted_iota(jnp.int32, (count, row.shape[1]), 0) + first
    return jnp.where(ids == row, 1.0, 0.0).astype(bf16)


def columns(row):
    k = row.shape[1]
    parts = [
        jnp.transpose(jnp.broadcast_to(row[:, i : i + 128], (128, 128))) for i in range(0, k, 128)
    ]
    return jnp.concatenate(parts, axis=0)


def one_hot(column, first, count):
    lane = lax.broadcasted_iota(jnp.int32, column.shape, 1)
    parts = [
        jnp.where(column == lane + (first + i), 1.0, 0.0).astype(bf16)
        for i in range(0, count, 128)
    ]
    return jnp.concatenate(parts, axis=1)


def sigmoid(value):
    return 0.5 * jnp.tanh(0.5 * value) + 0.5


def normalise(value, live=None):
    center = value - jnp.mean(value, axis=-1, keepdims=True)
    recip = lax.rsqrt(jnp.mean(center * center, axis=-1, keepdims=True) + epsilon)
    if live is not None:
        recip = jnp.where(live, recip, 0.0)
    return center * recip, recip


def norm_backward(upper, normed, recip):
    return recip * (
        upper
        - jnp.mean(upper, axis=-1, keepdims=True)
        - normed * jnp.mean(upper * normed, axis=-1, keepdims=True)
    )


def send_kernel(rows_ref, nodes_ref, out_hbm, out_ref, sems):
    n = nodes_ref.shape[0]
    regions, cap = rows_ref.shape
    listed = jnp.transpose(rows_ref[...])
    lane = lax.broadcasted_iota(jnp.int32, (cap, n), 1)
    pieces = sems.shape[0]
    group = regions // pieces
    copies = []
    for p in range(pieces):
        picks = jnp.concatenate(
            [
                jnp.where(listed[:, q : q + 1] == lane, 1.0, 0.0).astype(bf16)
                for q in range(p * group, (p + 1) * group)
            ],
            axis=0,
        )
        at = pl.ds(p * group * cap, group * cap)
        out_ref[at, :] = mm(picks, nodes_ref[...]).astype(bf16)
        copies.append(pltpu.make_async_copy(out_ref.at[at], out_hbm.at[at], sems.at[p]))
        copies[-1].start()
    for copy in copies:
        copy.wait()


def marks_of(remote, n, width):
    return (remote, remote + n, remote + n + width, remote + n + 2 * width)


def before_kernel(
    snd_ref,
    rcv_ref,
    edges_ref,
    nodes_ref,
    ein_ref,
    ebias_ref,
    eout_ref,
    nin_ref,
    nout_ref,
    out_ref,
    table_scr,
):
    n, width = nodes_ref.shape
    chunk = out_ref.shape[0]
    remote = out_ref.shape[1] - n - 2 * width - 3 * (width // 2)
    half = width // 2
    marks = marks_of(remote, n, width)
    c = pl.program_id(0)

    @pl.when(c == 0)
    def _():
        table_scr[...] = mm(nodes_ref[...], ein_ref[2 * width :, :]).astype(bf16)

    snd = columns(snd_ref[pl.ds(c, 1), :])
    near = one_hot(columns(rcv_ref[pl.ds(c, 1), :]), 0, n)
    out_ref[:, :remote] = one_hot(snd, n, remote)
    out_ref[:, marks[0] : marks[1]] = near
    out_ref[:, marks[1] : marks[2]] = mm(one_hot(snd, 0, n), nodes_ref[...]).astype(bf16)
    out_ref[:, marks[2] : marks[3]] = (
        mm(edges_ref[...], ein_ref[:width, :]) + mm(near, table_scr[...]) + ebias_ref[...]
    ).astype(bf16)
    weights = out_ref.at[:, pl.ds(marks[3], 3 * half)]

    @pl.when(c == 0)
    def _():
        weights[:, :half] = nin_ref[:, :half]
        for k, ref in ((1, eout_ref), (2, ein_ref.at[pl.ds(width, width)])):
            weights[:width, k * half : (k + 1) * half] = ref[:, :half]
            weights[width:, k * half : (k + 1) * half] = ref[:, half:]

    @pl.when(c == 1)
    def _():
        weights[:, :half] = nin_ref[:, half:]
        for k, ref in ((1, nout_ref), (2, ein_ref.at[pl.ds(2 * width, width)])):
            weights[:width, k * half : (k + 1) * half] = ref[:, :half]
            weights[width:, k * half : (k + 1) * half] = ref[:, half:]


def deal(core, mats_ref, vecs, mine_ref, send_ref):
    blocks = mine_ref.shape[0]
    regions = 2 * blocks
    share, width = mats_ref.shape[0] // regions, mats_ref.shape[1]
    tail = jnp.concatenate(
        [vec[:, j : j + 128] for vec in vecs for j in range(0, width, 128)], axis=0
    ).astype(bf16)
    for out_ref, parity in ((mine_ref, core), (send_ref, 1 - core)):
        for i in range(blocks):
            at = pl.multiple_of((2 * i + parity) * share, 16)
            rows = mats_ref[pl.ds(at, share), :]
            for j in range(width // 128):
                out_ref[i, j * share : (j + 1) * share] = rows[:, j * 128 : (j + 1) * 128]
            out_ref[i, width // 128 * share :] = tail


def main_kernel(
    place_ref,
    live_ref,
    egain_ref,
    nbias_ref,
    ngain_ref,
    arrived_ref,
    ready_hbm,
    cot_hbm,
    edges_hbm,
    nodes_hbm,
    ncot_hbm,
    hg_ref,
    base_ref,
    mine_ref,
    send_ref,
    part_ref,
    far_ref,
    x_ref,
    cot_ref,
    node_in_ref,
    ncot_ref,
    ws_ref,
    wr_ref,
    eout_ref,
    nin_ref,
    nout_ref,
    act_ref,
    slope_ref,
    normed_ref,
    recip_ref,
    mats_ref,
    pg_ref,
    chunk_sems,
    sems,
):
    count, width = part_ref.shape
    n = ncot_ref.shape[0]
    chunk = min(CHUNK, count)
    n_chunks = count // chunk
    remote = far_ref.shape[1]
    half = width // 2
    marks = marks_of(remote, n, width)
    streams = [
        (ready_hbm.at[:, pl.ds(0, remote)], far_ref),
        (ready_hbm.at[:, pl.ds(marks[1], width)], x_ref.at[:, pl.ds(width, width)]),
        (ready_hbm.at[:, pl.ds(marks[2], width)], part_ref),
        (ready_hbm.at[:, pl.ds(marks[0], n)], x_ref.at[:, pl.ds(2 * width, n)]),
        (cot_hbm, cot_ref),
        (edges_hbm, x_ref.at[:, pl.ds(0, width)]),
    ]

    def stream(k, c):
        src, dst = streams[k]
        at = pl.ds(c * chunk, chunk)
        return pltpu.make_async_copy(src.at[at], dst.at[at], chunk_sems.at[k, c])

    def halves(k, first, ref):
        size = ref.shape[0]
        return [
            (
                ready_hbm.at[pl.ds(first + h * size, size), pl.ds(marks[3] + k * half, half)],
                ref.at[:, pl.ds(h * half, half)],
            )
            for h in range(2)
        ]

    singles = (
        halves(2, 0, ws_ref)
        + halves(1, 0, eout_ref)
        + [(nodes_hbm, node_in_ref.at[:, pl.ds(0, width)])]
        + halves(0, 0, nin_ref)
        + halves(1, 2 * width, nout_ref)
        + [(ncot_hbm, ncot_ref)]
        + halves(2, 2 * width, wr_ref)
    )
    single = [pltpu.make_async_copy(src, dst, sems.at[k]) for k, (src, dst) in enumerate(singles)]
    stream(0, 0).start()
    stream(1, 0).start()
    single[0].start()
    single[1].start()
    stream(2, 0).start()
    single[2].start()
    single[3].start()
    for c in range(1, n_chunks):
        for k in range(3):
            stream(k, c).start()
    for c in range(n_chunks):
        stream(3, c).start()
    for k in range(4, 10):
        single[k].start()
    for c in range(n_chunks):
        for k in range(4, 6):
            stream(k, c).start()
    single[10].start()
    single[11].start()

    egain = egain_ref[...]

    def rows_at(c):
        return pl.ds(c * chunk, chunk)

    def pick(c):
        here = rows_at(c)
        x_ref[here, width : 2 * width] += mm(far_ref[here, :], arrived_ref[...]).astype(bf16)

    def activate(c):
        here = rows_at(c)
        hidden = part_ref[here, :] + mm(x_ref[here, width : 2 * width], ws_ref[...])
        s = sigmoid(hidden)
        act_ref[here, :] = (hidden * s).astype(bf16)
        slope_ref[here, :] = (s * (1.0 + hidden * (1.0 - s))).astype(KEPT)

    def send_message(c):
        here = rows_at(c)
        live = lax.broadcasted_iota(jnp.int32, (chunk, 1), 0) + c * chunk < live_ref[0]
        normed, recip = normalise(mm(act_ref[here, :], eout_ref[...]), live)
        normed_ref[here, :] = normed.astype(KEPT)
        recip_ref[here, :] = recip
        pg_ref[here, :] = (normed * egain).astype(bf16)

    def skewed(stages, before):
        for t in range(n_chunks + len(stages) - 1):
            for k in range(len(stages)):
                if 0 <= t - k < n_chunks:
                    before[k](t - k)
            for k in reversed(range(len(stages))):
                if 0 <= t - k < n_chunks:
                    stages[k](t - k)

    def nothing(c):
        pass

    def wait_pick(c):
        stream(0, c).wait()
        stream(1, c).wait()

    def wait_activate(c):
        stream(2, c).wait()
        if c == 0:
            single[0].wait()
            single[1].wait()

    def wait_message(c):
        if c == 0:
            single[2].wait()
            single[3].wait()

    skewed([pick, activate, send_message], [wait_pick, wait_activate, wait_message])
    for c in range(n_chunks):
        stream(3, c).wait()
    agg = mm_tn(x_ref[:, 2 * width :], pg_ref[...])

    for k in range(4, 10):
        single[k].wait()
    node_in_ref[:, width:] = agg.astype(bf16)
    node_in = node_in_ref[...]
    nodes = node_in_ref[:, :width]
    hidden = mm(node_in, nin_ref[...]) + nbias_ref[...]
    s = sigmoid(hidden)
    act = (hidden * s).astype(bf16)
    normed, recip = normalise(mm(act, nout_ref[...]))
    upstream = ncot_ref[...].astype(f32)
    pre_grad = norm_backward(upstream * ngain_ref[...], normed, recip).astype(bf16)
    hidden_grad = (mm_nt(pre_grad, nout_ref[...]) * (s * (1.0 + hidden * (1.0 - s)))).astype(bf16)
    node_in_grad = mm_nt(hidden_grad, nin_ref[...])
    agg_grad = node_in_grad[:, width:].astype(bf16)
    vecs = [
        None,
        None,
        jnp.sum(hidden_grad.astype(f32), axis=0, keepdims=True),
        jnp.sum(upstream * normed, axis=0, keepdims=True),
    ]

    def take_gradient(c):
        here = rows_at(c)
        message_grad = cot_ref[here, :].astype(f32) + mm(x_ref[here, 2 * width :], agg_grad)
        edge_normed = normed_ref[here, :].astype(f32)
        term = jnp.sum(message_grad * edge_normed, axis=0, keepdims=True)
        vecs[1] = term if c == 0 else vecs[1] + term
        pg_ref[here, :] = norm_backward(
            message_grad * egain, edge_normed, recip_ref[here, :]
        ).astype(bf16)

    def pass_gradient(c):
        here = rows_at(c)
        edge_grad = (mm_nt(pg_ref[here, :], eout_ref[...]) * slope_ref[here, :].astype(f32)).astype(bf16)
        hg_ref[here, :] = edge_grad
        term = jnp.sum(edge_grad.astype(f32), axis=0, keepdims=True)
        vecs[0] = term if c == 0 else vecs[0] + term

    def wait_take(c):
        stream(4, c).wait()

    skewed([take_gradient, pass_gradient], [wait_take, nothing])
    for c in range(n_chunks):
        stream(5, c).wait()
    by_inputs = mm_tn(x_ref[...], hg_ref[...])

    single[10].wait()
    single[11].wait()
    received = by_inputs[2 * width :].astype(bf16)
    base_ref[...] = (
        upstream + node_in_grad[:, :width] + mm_nt(received, wr_ref[...])
    )
    mats_ref[: 2 * width, :] = by_inputs[: 2 * width].astype(bf16)
    mats_ref[2 * width : 3 * width, :] = mm_tn(nodes, received).astype(bf16)
    mats_ref[3 * width : 4 * width, :] = mm_tn(act_ref[...], pg_ref[...]).astype(bf16)
    mats_ref[4 * width : 6 * width, :] = mm_tn(node_in, hidden_grad).astype(bf16)
    mats_ref[6 * width :, :] = mm_tn(act, pre_grad).astype(bf16)
    deal(place_ref[0], mats_ref, vecs, mine_ref, send_ref)


def senders_kernel(snd_ref, hg_ref, ws_ref, base_ref, sent_ref, out_ref):
    n, width = base_ref.shape
    remote = sent_ref.shape[0]
    snd = snd_ref[...]
    local = mm(one_hot_t(snd, 0, n), hg_ref[...]).astype(bf16)
    out_ref[...] = base_ref[...] + mm_nt(local, ws_ref[...])
    tile = 256 if remote % 256 == 0 else remote

    @pl.loop(0, remote // tile)
    def _(i):
        at = pl.multiple_of(i * tile, tile)
        part = mm(one_hot_t(snd, n + at, tile), hg_ref[...]).astype(bf16)
        sent_ref[pl.ds(at, tile), :] = part


def edges_kernel(hg_ref, cot_ref, w_ref, out_ref):
    out_ref[...] = (cot_ref[...].astype(f32) + mm_nt(hg_ref[...], w_ref[...])).astype(bf16)


def finish_kernel(rows_ref, returned_ref, ws_ref, base_ref, out_ref):
    n, width = base_ref.shape
    own = mm(one_hot_t(rows_ref[...], 0, n), returned_ref[...]).astype(bf16)
    out_ref[...] = (base_ref[...] + mm_nt(own, ws_ref[...])).astype(bf16)


def over_chips_kernel(parts_ref, own_ref, sent_ref):
    total = jnp.sum(parts_ref[...].astype(f32), axis=0)
    own_ref[...] = total
    sent_ref[...] = total.astype(bf16)


def join_kernel(*refs):
    mats_ref, vecs_ref = refs[-2:]
    share, width = mats_ref.shape
    total = refs[0][...]
    for ref in refs[1:-2]:
        total = total + ref[...].astype(f32)
    slabs = width // 128
    for j in range(slabs):
        mats_ref[:, j * 128 : (j + 1) * 128] = total[j * share : (j + 1) * share]
        for k in range(4):
            at = slabs * share + k * slabs + j
            vecs_ref[k : k + 1, j * 128 : (j + 1) * 128] = total[at : at + 1]


def shards(
    node_feat,
    edge_feat,
    node_cot,
    edge_cot,
    edge_in_w,
    edge_bias,
    edge_out_w,
    edge_gain,
    node_in_w,
    node_bias,
    node_out_w,
    node_gain,
    senders,
    receivers,
    send_rows,
    live_edges,
):
    nodes = node_feat[0]
    edges = edge_feat[0]
    cots = edge_cot[0]
    n, width = nodes.shape
    count = edges.shape[0]
    regions, cap = send_rows.shape
    remote = regions * cap
    chunk = min(CHUNK, count)
    n_chunks = count // chunk
    rows = edge_in_w.shape[0] + edge_out_w.shape[0] + node_in_w.shape[0] + node_out_w.shape[0]
    share = rows // regions
    chips = regions // 2
    reps = lax.axis_size("rep")
    core = lax.rem(lax.axis_index("dom"), 2).reshape(1)
    smem = pl.BlockSpec(memory_space=pltpu.SMEM)
    vmem = pl.BlockSpec(memory_space=pltpu.VMEM)
    hbm = pl.BlockSpec(memory_space=pl.ANY)
    shape = jax.ShapeDtypeStruct

    def whole(shape):
        return pl.BlockSpec(shape, lambda i: (0,) * len(shape))

    def rows_of(width):
        return pl.BlockSpec((chunk, width), lambda i: (i, 0))

    outgoing = pl.pallas_call(
        send_kernel,
        out_specs=hbm,
        out_shape=shape((remote, width), bf16),
        scratch_shapes=[
            pltpu.VMEM((remote, width), bf16),
            pltpu.SemaphoreType.DMA((2,)),
        ],
        compiler_params=params(58),
        cost_estimate=cost(2 * remote * n * width, 4 * remote * width),
    )(send_rows, nodes)
    arrived = lax.all_to_all(
        outgoing.reshape(regions, cap, width), "dom", split_axis=0, concat_axis=0, tiled=True
    ).reshape(remote, width)

    assert n_chunks == 2 and chunk == 2 * width
    columns_in_all = marks_of(remote, n, width)[3] + 3 * (width // 2)
    ready = pl.pallas_call(
        before_kernel,
        grid=(n_chunks,),
        in_specs=[
            whole((n_chunks, chunk)),
            whole((n_chunks, chunk)),
            rows_of(width),
            whole((n, width)),
            whole(edge_in_w.shape),
            whole((1, width)),
            whole(edge_out_w.shape),
            whole(node_in_w.shape),
            whole(node_out_w.shape),
        ],
        out_specs=rows_of(columns_in_all),
        out_shape=shape((count, columns_in_all), bf16),
        scratch_shapes=[pltpu.VMEM((n, width), bf16)],
        compiler_params=params(BEFORE_LIMIT),
        cost_estimate=cost(6_000_000_000, 16_000_000),
    )(
        senders.reshape(n_chunks, chunk),
        receivers.reshape(n_chunks, chunk),
        edges,
        nodes,
        edge_in_w,
        edge_bias.reshape(1, width),
        edge_out_w,
        node_in_w,
        node_out_w,
    )

    slab = (share * width + 4 * width) // 128
    dealt = (chips, slab, 128)
    hidden_grad, base, mine, to_other = pl.pallas_call(
        main_kernel,
        in_specs=[smem] * 2 + [vmem] * 4 + [hbm] * 5,
        out_specs=[vmem] * 4,
        out_shape=[
            shape((count, width), bf16),
            shape((n, width), f32),
            shape(dealt, bf16),
            shape(dealt, bf16),
        ],
        scratch_shapes=[
            pltpu.VMEM((count, width), bf16),
            pltpu.VMEM((count, remote), bf16),
            pltpu.VMEM((count, 2 * width + n), bf16),
            pltpu.VMEM((count, width), bf16),
            pltpu.VMEM((n, 2 * width), bf16),
            pltpu.VMEM((n, width), bf16),
            pltpu.VMEM((width, width), bf16),
            pltpu.VMEM((width, width), bf16),
            pltpu.VMEM(edge_out_w.shape, bf16),
            pltpu.VMEM(node_in_w.shape, bf16),
            pltpu.VMEM(node_out_w.shape, bf16),
            pltpu.VMEM((count, width), bf16),
            pltpu.VMEM((count, width), KEPT),
            pltpu.VMEM((count, width), KEPT),
            pltpu.VMEM((count, 1), f32),
            pltpu.VMEM((rows, width), bf16),
            pltpu.VMEM((count, width), bf16),
            pltpu.SemaphoreType.DMA((6, n_chunks)),
            pltpu.SemaphoreType.DMA((12,)),
        ],
        compiler_params=params(MAIN_LIMIT),
        cost_estimate=cost(16_000_000_000, 30_000_000),
    )(
        core,
        live_edges,
        edge_gain.reshape(1, width),
        node_bias.reshape(1, width),
        node_gain.reshape(1, width),
        arrived,
        ready,
        cots,
        edges,
        nodes,
        node_cot[0],
    )

    w_s = edge_in_w[width : 2 * width]
    from_other = lax.ppermute(to_other, "dom", [(i, i ^ 1) for i in range(regions)])
    chip_sum = (mine.astype(f32) + from_other.astype(f32)).astype(bf16)
    chip_sum, hidden_grad = lax.optimization_barrier((chip_sum, hidden_grad))
    by_chip = lax.all_to_all(
        chip_sum,
        "dom",
        split_axis=0,
        concat_axis=0,
        axis_index_groups=[list(range(c, regions, 2)) for c in range(2)],
        tiled=True,
    )
    sent, base = pl.pallas_call(
        senders_kernel,
        out_shape=(shape((remote, width), bf16), shape((n, width), f32)),
        compiler_params=params(),
        cost_estimate=cost(1000, 1000),
    )(senders.reshape(1, count), hidden_grad, w_s, base)
    grad_edges = pl.pallas_call(
        edges_kernel,
        grid=(n_chunks,),
        in_specs=[
            rows_of(width),
            rows_of(width),
            pl.BlockSpec((width, width), lambda i: (0, 0)),
        ],
        out_specs=rows_of(width),
        out_shape=shape((count, width), bf16),
        compiler_params=params(),
        cost_estimate=cost(1000, 1000),
    )(hidden_grad, cots, edge_in_w)

    by_chip, sent, grad_edges = lax.optimization_barrier((by_chip, sent, grad_edges))
    returned = lax.all_to_all(
        sent.reshape(regions, cap, width), "dom", split_axis=0, concat_axis=0, tiled=True
    ).reshape(remote, width)
    total, total_bf16 = pl.pallas_call(
        over_chips_kernel,
        out_shape=(shape((slab, 128), f32), shape((slab, 128), bf16)),
        compiler_params=params(),
        cost_estimate=cost(1_000_000, 2_000_000),
    )(by_chip)
    totals = [total] + [
        lax.ppermute(total_bf16, "rep", [(i, (i + k) % reps) for i in range(reps)])
        for k in range(1, reps)
    ]
    grad_nodes = pl.pallas_call(
        finish_kernel,
        out_shape=shape((n, width), bf16),
        compiler_params=params(),
        cost_estimate=cost(1000, 1000),
    )(send_rows.reshape(1, remote), returned, w_s, base)
    own_rows, vector_total = pl.pallas_call(
        join_kernel,
        out_shape=(shape((share, width), f32), shape((4, width), f32)),
        compiler_params=params(),
    )(*totals)
    return (grad_nodes[None], grad_edges[None], own_rows, vector_total)


def solution(mesh):
    in_specs = (
        P("rep", "dom", None),
        P("rep", "dom", None),
        P("rep", "dom", None),
        P("rep", "dom", None),
        P(),
        P(),
        P(),
        P(),
        P(),
        P(),
        P(),
        P(),
        P("dom"),
        P("dom"),
        P("dom", None),
        P("dom"),
    )
    out_specs = (P("rep", "dom", None), P("rep", "dom", None), P("dom", None), P())
    return jax.shard_map(shards, mesh=mesh, in_specs=in_specs, out_specs=out_specs, check_vma=False)
```

```python
import jax
import jax.numpy as jnp
from jax import lax
from jax.experimental import pallas as pl
from jax.experimental.pallas import tpu as pltpu
from jax.sharding import PartitionSpec as P

epsilon = 1e-05
f32 = jnp.float32
bf16 = jnp.bfloat16
NT = (((1,), (1,)), ((), ()))
TN = (((0,), (0,)), ((), ()))
MAIN_LIMIT = 48
BEFORE_LIMIT = 60
CHUNK = 1024
KEPT = bf16


def mm(a, b):
    return jnp.dot(a, b, preferred_element_type=f32)


def mm_nt(a, b):
    return lax.dot_general(a, b, NT, preferred_element_type=f32)


def mm_tn(a, b):
    return lax.dot_general(a, b, TN, preferred_element_type=f32)


def params(limit=16):
    return pltpu.CompilerParams(vmem_limit_bytes=limit * 1024 * 1024)


def cost(flops, moved):
    return pl.CostEstimate(flops=flops, bytes_accessed=moved, transcendentals=0)


def one_hot_t(row, first, count):
    ids = lax.broadcasted_iota(jnp.int32, (count, row.shape[1]), 0) + first
    return jnp.where(ids == row, 1.0, 0.0).astype(bf16)


def columns(row):
    k = row.shape[1]
    parts = [
        jnp.transpose(jnp.broadcast_to(row[:, i : i + 128], (128, 128))) for i in range(0, k, 128)
    ]
    return jnp.concatenate(parts, axis=0)


def one_hot(column, first, count):
    lane = lax.broadcasted_iota(jnp.int32, column.shape, 1)
    parts = [
        jnp.where(column == lane + (first + i), 1.0, 0.0).astype(bf16)
        for i in range(0, count, 128)
    ]
    return jnp.concatenate(parts, axis=1)


def sigmoid(value):
    return 1.0 / (1.0 + jnp.exp(-value))


def normalise(value, live=None):
    center = value - jnp.mean(value, axis=-1, keepdims=True)
    recip = lax.rsqrt(jnp.mean(center * center, axis=-1, keepdims=True) + epsilon)
    if live is not None:
        recip = jnp.where(live, recip, 0.0)
    return center * recip, recip


def norm_backward(upper, normed, recip):
    return recip * (
        upper
        - jnp.mean(upper, axis=-1, keepdims=True)
        - normed * jnp.mean(upper * normed, axis=-1, keepdims=True)
    )


def send_kernel(rows_ref, nodes_ref, out_hbm, out_ref, sems):
    n = nodes_ref.shape[0]
    regions, cap = rows_ref.shape
    listed = jnp.transpose(rows_ref[...])
    lane = lax.broadcasted_iota(jnp.int32, (cap, n), 1)
    pieces = sems.shape[0]
    group = regions // pieces
    copies = []
    for p in range(pieces):
        picks = jnp.concatenate(
            [
                jnp.where(listed[:, q : q + 1] == lane, 1.0, 0.0).astype(bf16)
                for q in range(p * group, (p + 1) * group)
            ],
            axis=0,
        )
        at = pl.ds(p * group * cap, group * cap)
        out_ref[at, :] = mm(picks, nodes_ref[...]).astype(bf16)
        copies.append(pltpu.make_async_copy(out_ref.at[at], out_hbm.at[at], sems.at[p]))
        copies[-1].start()
    for copy in copies:
        copy.wait()


def marks_of(remote, n, width):
    return (remote, remote + n, remote + n + width, remote + n + 2 * width)


def before_kernel(
    snd_ref,
    rcv_ref,
    edges_ref,
    nodes_ref,
    ein_ref,
    ebias_ref,
    eout_ref,
    nin_ref,
    nout_ref,
    out_ref,
    table_scr,
):
    n, width = nodes_ref.shape
    chunk = out_ref.shape[0]
    remote = out_ref.shape[1] - n - 2 * width - 3 * (width // 2)
    half = width // 2
    marks = marks_of(remote, n, width)
    c = pl.program_id(0)

    @pl.when(c == 0)
    def _():
        table_scr[...] = mm(nodes_ref[...], ein_ref[2 * width :, :]).astype(bf16)

    snd = columns(snd_ref[pl.ds(c, 1), :])
    near = one_hot(columns(rcv_ref[pl.ds(c, 1), :]), 0, n)
    out_ref[:, :remote] = one_hot(snd, n, remote)
    out_ref[:, marks[0] : marks[1]] = near
    out_ref[:, marks[1] : marks[2]] = mm(one_hot(snd, 0, n), nodes_ref[...]).astype(bf16)
    out_ref[:, marks[2] : marks[3]] = (
        mm(edges_ref[...], ein_ref[:width, :]) + mm(near, table_scr[...]) + ebias_ref[...]
    ).astype(bf16)
    weights = out_ref.at[:, pl.ds(marks[3], 3 * half)]

    @pl.when(c == 0)
    def _():
        weights[:, :half] = nin_ref[:, :half]
        for k, ref in ((1, eout_ref), (2, ein_ref.at[pl.ds(width, width)])):
            weights[:width, k * half : (k + 1) * half] = ref[:, :half]
            weights[width:, k * half : (k + 1) * half] = ref[:, half:]

    @pl.when(c == 1)
    def _():
        weights[:, :half] = nin_ref[:, half:]
        for k, ref in ((1, nout_ref), (2, ein_ref.at[pl.ds(2 * width, width)])):
            weights[:width, k * half : (k + 1) * half] = ref[:, :half]
            weights[width:, k * half : (k + 1) * half] = ref[:, half:]


def deal(core, mats_ref, vecs, mine_ref, send_ref):
    blocks = mine_ref.shape[0]
    regions = 2 * blocks
    share, width = mats_ref.shape[0] // regions, mats_ref.shape[1]
    tail = jnp.concatenate(
        [vec[:, j : j + 128] for vec in vecs for j in range(0, width, 128)], axis=0
    ).astype(bf16)
    for out_ref, parity in ((mine_ref, core), (send_ref, 1 - core)):
        for i in range(blocks):
            at = pl.multiple_of((2 * i + parity) * share, 16)
            rows = mats_ref[pl.ds(at, share), :]
            for j in range(width // 128):
                out_ref[i, j * share : (j + 1) * share] = rows[:, j * 128 : (j + 1) * 128]
            out_ref[i, width // 128 * share :] = tail


def main_kernel(
    place_ref,
    live_ref,
    egain_ref,
    nbias_ref,
    ngain_ref,
    arrived_ref,
    ready_hbm,
    cot_hbm,
    edges_hbm,
    nodes_hbm,
    ncot_hbm,
    hg_ref,
    base_ref,
    mine_ref,
    send_ref,
    part_ref,
    far_ref,
    x_ref,
    cot_ref,
    node_in_ref,
    ncot_ref,
    ws_ref,
    wr_ref,
    eout_ref,
    nin_ref,
    nout_ref,
    act_ref,
    slope_ref,
    normed_ref,
    recip_ref,
    mats_ref,
    pg_ref,
    chunk_sems,
    sems,
):
    count, width = part_ref.shape
    n = ncot_ref.shape[0]
    chunk = min(CHUNK, count)
    n_chunks = count // chunk
    remote = far_ref.shape[1]
    half = width // 2
    marks = marks_of(remote, n, width)
    streams = [
        (ready_hbm.at[:, pl.ds(0, remote)], far_ref),
        (ready_hbm.at[:, pl.ds(marks[1], width)], x_ref.at[:, pl.ds(width, width)]),
        (ready_hbm.at[:, pl.ds(marks[2], width)], part_ref),
        (ready_hbm.at[:, pl.ds(marks[0], n)], x_ref.at[:, pl.ds(2 * width, n)]),
        (cot_hbm, cot_ref),
        (edges_hbm, x_ref.at[:, pl.ds(0, width)]),
    ]

    def stream(k, c):
        src, dst = streams[k]
        at = pl.ds(c * chunk, chunk)
        return pltpu.make_async_copy(src.at[at], dst.at[at], chunk_sems.at[k, c])

    def halves(k, first, ref):
        size = ref.shape[0]
        return [
            (
                ready_hbm.at[pl.ds(first + h * size, size), pl.ds(marks[3] + k * half, half)],
                ref.at[:, pl.ds(h * half, half)],
            )
            for h in range(2)
        ]

    singles = (
        halves(2, 0, ws_ref)
        + halves(1, 0, eout_ref)
        + [(nodes_hbm, node_in_ref.at[:, pl.ds(0, width)])]
        + halves(0, 0, nin_ref)
        + halves(1, 2 * width, nout_ref)
        + [(ncot_hbm, ncot_ref)]
        + halves(2, 2 * width, wr_ref)
    )
    single = [pltpu.make_async_copy(src, dst, sems.at[k]) for k, (src, dst) in enumerate(singles)]
    stream(0, 0).start()
    stream(1, 0).start()
    single[0].start()
    single[1].start()
    stream(2, 0).start()
    single[2].start()
    single[3].start()
    for c in range(1, n_chunks):
        for k in range(3):
            stream(k, c).start()
    for c in range(n_chunks):
        stream(3, c).start()
    for k in range(4, 10):
        single[k].start()
    for c in range(n_chunks):
        for k in range(4, 6):
            stream(k, c).start()
    single[10].start()
    single[11].start()

    egain = egain_ref[...]

    def rows_at(c):
        return pl.ds(c * chunk, chunk)

    def pick(c):
        here = rows_at(c)
        x_ref[here, width : 2 * width] += mm(far_ref[here, :], arrived_ref[...]).astype(bf16)

    def activate(c):
        here = rows_at(c)
        hidden = part_ref[here, :] + mm(x_ref[here, width : 2 * width], ws_ref[...])
        s = sigmoid(hidden)
        act_ref[here, :] = (hidden * s).astype(bf16)
        slope_ref[here, :] = (s * (1.0 + hidden * (1.0 - s))).astype(KEPT)

    def send_message(c):
        here = rows_at(c)
        live = lax.broadcasted_iota(jnp.int32, (chunk, 1), 0) + c * chunk < live_ref[0]
        normed, recip = normalise(mm(act_ref[here, :], eout_ref[...]), live)
        normed_ref[here, :] = normed.astype(KEPT)
        recip_ref[here, :] = recip
        pg_ref[here, :] = (normed * egain).astype(bf16)

    def skewed(stages, before):
        for t in range(n_chunks + len(stages) - 1):
            for k in range(len(stages)):
                if 0 <= t - k < n_chunks:
                    before[k](t - k)
            for k in reversed(range(len(stages))):
                if 0 <= t - k < n_chunks:
                    stages[k](t - k)

    def nothing(c):
        pass

    def wait_pick(c):
        stream(0, c).wait()
        stream(1, c).wait()

    def wait_activate(c):
        stream(2, c).wait()
        if c == 0:
            single[0].wait()
            single[1].wait()

    def wait_message(c):
        if c == 0:
            single[2].wait()
            single[3].wait()

    skewed([pick, activate, send_message], [wait_pick, wait_activate, wait_message])
    for c in range(n_chunks):
        stream(3, c).wait()
    agg = mm_tn(x_ref[:, 2 * width :], pg_ref[...])

    for k in range(4, 10):
        single[k].wait()
    node_in_ref[:, width:] = agg.astype(bf16)
    node_in = node_in_ref[...]
    nodes = node_in_ref[:, :width]
    hidden = mm(node_in, nin_ref[...]) + nbias_ref[...]
    s = sigmoid(hidden)
    act = (hidden * s).astype(bf16)
    normed, recip = normalise(mm(act, nout_ref[...]))
    upstream = ncot_ref[...].astype(f32)
    pre_grad = norm_backward(upstream * ngain_ref[...], normed, recip).astype(bf16)
    hidden_grad = (mm_nt(pre_grad, nout_ref[...]) * (s * (1.0 + hidden * (1.0 - s)))).astype(bf16)
    node_in_grad = mm_nt(hidden_grad, nin_ref[...])
    agg_grad = node_in_grad[:, width:].astype(bf16)
    vecs = [
        None,
        None,
        jnp.sum(hidden_grad.astype(f32), axis=0, keepdims=True),
        jnp.sum(upstream * normed, axis=0, keepdims=True),
    ]

    def take_gradient(c):
        here = rows_at(c)
        message_grad = cot_ref[here, :].astype(f32) + mm(x_ref[here, 2 * width :], agg_grad)
        edge_normed = normed_ref[here, :].astype(f32)
        term = jnp.sum(message_grad * edge_normed, axis=0, keepdims=True)
        vecs[1] = term if c == 0 else vecs[1] + term
        pg_ref[here, :] = norm_backward(
            message_grad * egain, edge_normed, recip_ref[here, :]
        ).astype(bf16)

    def pass_gradient(c):
        here = rows_at(c)
        edge_grad = (mm_nt(pg_ref[here, :], eout_ref[...]) * slope_ref[here, :].astype(f32)).astype(bf16)
        hg_ref[here, :] = edge_grad
        term = jnp.sum(edge_grad.astype(f32), axis=0, keepdims=True)
        vecs[0] = term if c == 0 else vecs[0] + term

    def wait_take(c):
        stream(4, c).wait()

    skewed([take_gradient, pass_gradient], [wait_take, nothing])
    for c in range(n_chunks):
        stream(5, c).wait()
    by_inputs = mm_tn(x_ref[...], hg_ref[...])

    single[10].wait()
    single[11].wait()
    received = by_inputs[2 * width :].astype(bf16)
    base_ref[...] = (
        upstream + node_in_grad[:, :width] + mm_nt(received, wr_ref[...])
    )
    mats_ref[: 2 * width, :] = by_inputs[: 2 * width].astype(bf16)
    mats_ref[2 * width : 3 * width, :] = mm_tn(nodes, received).astype(bf16)
    mats_ref[3 * width : 4 * width, :] = mm_tn(act_ref[...], pg_ref[...]).astype(bf16)
    mats_ref[4 * width : 6 * width, :] = mm_tn(node_in, hidden_grad).astype(bf16)
    mats_ref[6 * width :, :] = mm_tn(act, pre_grad).astype(bf16)
    deal(place_ref[0], mats_ref, vecs, mine_ref, send_ref)


def senders_kernel(snd_ref, hg_ref, ws_ref, base_ref, sent_ref, out_ref):
    n, width = base_ref.shape
    remote = sent_ref.shape[0]
    snd = snd_ref[...]
    local = mm(one_hot_t(snd, 0, n), hg_ref[...]).astype(bf16)
    out_ref[...] = base_ref[...] + mm_nt(local, ws_ref[...])
    tile = 256 if remote % 256 == 0 else remote

    @pl.loop(0, remote // tile)
    def _(i):
        at = pl.multiple_of(i * tile, tile)
        part = mm(one_hot_t(snd, n + at, tile), hg_ref[...]).astype(bf16)
        sent_ref[pl.ds(at, tile), :] = part


def edges_kernel(hg_ref, cot_ref, w_ref, out_ref):
    out_ref[...] = (cot_ref[...].astype(f32) + mm_nt(hg_ref[...], w_ref[...])).astype(bf16)


def finish_kernel(rows_ref, returned_ref, ws_ref, base_ref, out_ref):
    n, width = base_ref.shape
    own = mm(one_hot_t(rows_ref[...], 0, n), returned_ref[...]).astype(bf16)
    out_ref[...] = (base_ref[...] + mm_nt(own, ws_ref[...])).astype(bf16)


def over_chips_kernel(parts_ref, own_ref, sent_ref):
    total = jnp.sum(parts_ref[...].astype(f32), axis=0)
    own_ref[...] = total
    sent_ref[...] = total.astype(bf16)


def join_kernel(*refs):
    mats_ref, vecs_ref = refs[-2:]
    share, width = mats_ref.shape
    total = refs[0][...]
    for ref in refs[1:-2]:
        total = total + ref[...].astype(f32)
    slabs = width // 128
    for j in range(slabs):
        mats_ref[:, j * 128 : (j + 1) * 128] = total[j * share : (j + 1) * share]
        for k in range(4):
            at = slabs * share + k * slabs + j
            vecs_ref[k : k + 1, j * 128 : (j + 1) * 128] = total[at : at + 1]


def shards(
    node_feat,
    edge_feat,
    node_cot,
    edge_cot,
    edge_in_w,
    edge_bias,
    edge_out_w,
    edge_gain,
    node_in_w,
    node_bias,
    node_out_w,
    node_gain,
    senders,
    receivers,
    send_rows,
    live_edges,
):
    nodes = node_feat[0]
    edges = edge_feat[0]
    cots = edge_cot[0]
    n, width = nodes.shape
    count = edges.shape[0]
    regions, cap = send_rows.shape
    remote = regions * cap
    chunk = min(CHUNK, count)
    n_chunks = count // chunk
    rows = edge_in_w.shape[0] + edge_out_w.shape[0] + node_in_w.shape[0] + node_out_w.shape[0]
    share = rows // regions
    chips = regions // 2
    reps = lax.axis_size("rep")
    core = lax.rem(lax.axis_index("dom"), 2).reshape(1)
    smem = pl.BlockSpec(memory_space=pltpu.SMEM)
    vmem = pl.BlockSpec(memory_space=pltpu.VMEM)
    hbm = pl.BlockSpec(memory_space=pl.ANY)
    shape = jax.ShapeDtypeStruct

    def whole(shape):
        return pl.BlockSpec(shape, lambda i: (0,) * len(shape))

    def rows_of(width):
        return pl.BlockSpec((chunk, width), lambda i: (i, 0))

    outgoing = pl.pallas_call(
        send_kernel,
        out_specs=hbm,
        out_shape=shape((remote, width), bf16),
        scratch_shapes=[
            pltpu.VMEM((remote, width), bf16),
            pltpu.SemaphoreType.DMA((2,)),
        ],
        compiler_params=params(58),
        cost_estimate=cost(2 * remote * n * width, 4 * remote * width),
    )(send_rows, nodes)
    arrived = lax.all_to_all(
        outgoing.reshape(regions, cap, width), "dom", split_axis=0, concat_axis=0, tiled=True
    ).reshape(remote, width)

    assert n_chunks == 2 and chunk == 2 * width
    columns_in_all = marks_of(remote, n, width)[3] + 3 * (width // 2)
    ready = pl.pallas_call(
        before_kernel,
        grid=(n_chunks,),
        in_specs=[
            whole((n_chunks, chunk)),
            whole((n_chunks, chunk)),
            rows_of(width),
            whole((n, width)),
            whole(edge_in_w.shape),
            whole((1, width)),
            whole(edge_out_w.shape),
            whole(node_in_w.shape),
            whole(node_out_w.shape),
        ],
        out_specs=rows_of(columns_in_all),
        out_shape=shape((count, columns_in_all), bf16),
        scratch_shapes=[pltpu.VMEM((n, width), bf16)],
        compiler_params=params(BEFORE_LIMIT),
        cost_estimate=cost(6_000_000_000, 16_000_000),
    )(
        senders.reshape(n_chunks, chunk),
        receivers.reshape(n_chunks, chunk),
        edges,
        nodes,
        edge_in_w,
        edge_bias.reshape(1, width),
        edge_out_w,
        node_in_w,
        node_out_w,
    )

    slab = (share * width + 4 * width) // 128
    dealt = (chips, slab, 128)
    hidden_grad, base, mine, to_other = pl.pallas_call(
        main_kernel,
        in_specs=[smem] * 2 + [vmem] * 4 + [hbm] * 5,
        out_specs=[vmem] * 4,
        out_shape=[
            shape((count, width), bf16),
            shape((n, width), f32),
            shape(dealt, bf16),
            shape(dealt, bf16),
        ],
        scratch_shapes=[
            pltpu.VMEM((count, width), bf16),
            pltpu.VMEM((count, remote), bf16),
            pltpu.VMEM((count, 2 * width + n), bf16),
            pltpu.VMEM((count, width), bf16),
            pltpu.VMEM((n, 2 * width), bf16),
            pltpu.VMEM((n, width), bf16),
            pltpu.VMEM((width, width), bf16),
            pltpu.VMEM((width, width), bf16),
            pltpu.VMEM(edge_out_w.shape, bf16),
            pltpu.VMEM(node_in_w.shape, bf16),
            pltpu.VMEM(node_out_w.shape, bf16),
            pltpu.VMEM((count, width), bf16),
            pltpu.VMEM((count, width), KEPT),
            pltpu.VMEM((count, width), KEPT),
            pltpu.VMEM((count, 1), f32),
            pltpu.VMEM((rows, width), bf16),
            pltpu.VMEM((count, width), bf16),
            pltpu.SemaphoreType.DMA((6, n_chunks)),
            pltpu.SemaphoreType.DMA((12,)),
        ],
        compiler_params=params(MAIN_LIMIT),
        cost_estimate=cost(16_000_000_000, 30_000_000),
    )(
        core,
        live_edges,
        edge_gain.reshape(1, width),
        node_bias.reshape(1, width),
        node_gain.reshape(1, width),
        arrived,
        ready,
        cots,
        edges,
        nodes,
        node_cot[0],
    )

    w_s = edge_in_w[width : 2 * width]
    from_other = lax.ppermute(to_other, "dom", [(i, i ^ 1) for i in range(regions)])
    chip_sum = (mine.astype(f32) + from_other.astype(f32)).astype(bf16)
    chip_sum, hidden_grad = lax.optimization_barrier((chip_sum, hidden_grad))
    by_chip = lax.all_to_all(
        chip_sum,
        "dom",
        split_axis=0,
        concat_axis=0,
        axis_index_groups=[list(range(c, regions, 2)) for c in range(2)],
        tiled=True,
    )
    sent, base = pl.pallas_call(
        senders_kernel,
        out_shape=(shape((remote, width), bf16), shape((n, width), f32)),
        compiler_params=params(),
        cost_estimate=cost(1000, 1000),
    )(senders.reshape(1, count), hidden_grad, w_s, base)
    grad_edges = pl.pallas_call(
        edges_kernel,
        grid=(n_chunks,),
        in_specs=[
            rows_of(width),
            rows_of(width),
            pl.BlockSpec((width, width), lambda i: (0, 0)),
        ],
        out_specs=rows_of(width),
        out_shape=shape((count, width), bf16),
        compiler_params=params(),
        cost_estimate=cost(1000, 1000),
    )(hidden_grad, cots, edge_in_w)

    by_chip, sent, grad_edges = lax.optimization_barrier((by_chip, sent, grad_edges))
    returned = lax.all_to_all(
        sent.reshape(regions, cap, width), "dom", split_axis=0, concat_axis=0, tiled=True
    ).reshape(remote, width)
    total, total_bf16 = pl.pallas_call(
        over_chips_kernel,
        out_shape=(shape((slab, 128), f32), shape((slab, 128), bf16)),
        compiler_params=params(),
        cost_estimate=cost(1_000_000, 2_000_000),
    )(by_chip)
    totals = [total] + [
        lax.ppermute(total_bf16, "rep", [(i, (i + k) % reps) for i in range(reps)])
        for k in range(1, reps)
    ]
    grad_nodes = pl.pallas_call(
        finish_kernel,
        out_shape=shape((n, width), bf16),
        compiler_params=params(),
        cost_estimate=cost(1000, 1000),
    )(send_rows.reshape(1, remote), returned, w_s, base)
    own_rows, vector_total = pl.pallas_call(
        join_kernel,
        out_shape=(shape((share, width), f32), shape((4, width), f32)),
        compiler_params=params(),
    )(*totals)
    return (grad_nodes[None], grad_edges[None], own_rows, vector_total)


def solution(mesh):
    in_specs = (
        P("rep", "dom", None),
        P("rep", "dom", None),
        P("rep", "dom", None),
        P("rep", "dom", None),
        P(),
        P(),
        P(),
        P(),
        P(),
        P(),
        P(),
        P(),
        P("dom"),
        P("dom"),
        P("dom", None),
        P("dom"),
    )
    out_specs = (P("rep", "dom", None), P("rep", "dom", None), P("dom", None), P())
    return jax.shard_map(shards, mesh=mesh, in_specs=in_specs, out_specs=out_specs, check_vma=False)
```
